32 devices in a mesh: gy: 4 (over x, core), gz: 8 (over z, y).
Axes of the slice: x: 2, y: 2, z: 4, core: 2. Of those that a mesh axis runs over, the one named last changes fastest.
Arguments:
- offsets: float32 [3, 262144], P(None, ('gy', 'gz')), may hold values from 0 to 1
- masses: float32 [262144], P(('gy', 'gz')), may hold values from 0.25 to 4
- velocities: float32 [3, 262144], P(None, ('gy', 'gz')), may hold values from -5 to 5
- destination: int32 [262144, 1], P(('gy', 'gz')), may hold values from 0 to 31; in each aligned block of 8192 rows (0 to 8191, 8192 to 16383, ...) at most 512 rows name the same one
- first_weight: bfloat16 [16, 4, 3, 3, 3], replicated, may hold values from -0.625 to 0.625
- first_bias: float32 [16], replicated, may hold values from -3 to 3
- second_weight: bfloat16 [16, 16, 3, 3, 3], replicated, may hold values from -0.3125 to 0.3125
- second_bias: float32 [16], replicated, may hold values from -3 to 3
- cotangent: bfloat16 [16, 32, 64, 128], P(None, 'gy', 'gz'), may hold values from -6 to 6
Outputs:
- refined: bfloat16 [16, 32, 64, 128], P(None, 'gy', 'gz')
- grad_field: float32 [4, 32, 64, 128], P(None, 'gy', 'gz')
- grad_first_weight: float32 [16, 4, 3, 3, 3], replicated
- grad_first_bias: float32 [16], replicated
- grad_second_weight: float32 [16, 16, 3, 3, 3], replicated
- grad_second_bias: float32 [16], replicated
The draws below stay inside these ranges and needn't reach their ends.
Inputs may be any that keep to these rules, and one draw needn't show every extreme that they name: `destination`: in the rows of one device (aligned blocks of 8192 rows) no block number is named by more than 512 rows, and some block number is named by exactly 512.
All inputs are finite; a program needn't handle non-finite values.
Results may differ from the reference program's by a relative error of at most 0.009.
Values may be sent and summed in bfloat16 or wider, within the bound.
No kernel may reach another device: no remote copies, remote signals or barrier semaphores. Data moves between devices by JAX's collectives and lax.ppermute only.
A program may use at most 192 MiB of HBM per device.

```python
import math
import jax
import jax.numpy as jnp
import numpy as np
from jax import lax

CH = 16
C_IN = 4
BY = 8
BZ = 8
NXW = 128
NY = 32
NZ = 64
PART_DEV = 8192
CAP = 512
PARTICLES = 262144
N_GZ = 8
DEVICES = 32


def level_of(stream_key, extent, cuts, smallest, high):
    loudness = 1.0
    for dim, parts in cuts:
        draws = jax.random.uniform(jax.random.fold_in(jax.random.fold_in(stream_key, 6), dim), (parts,), jnp.float32, smallest / len(cuts), high / len(cuts))
        loudness = loudness * jnp.repeat(jnp.exp(draws), extent[dim] // parts).reshape((-1,) + (1,) * (len(extent) - 1 - dim))
    return loudness


def deal_out(stream_key, own, number, rows, amount, top, reach, skew):
    sequence = jax.random.permutation(stream_key, amount)
    packed, ordinary = load_shares(amount, rows * top, reach, skew, True), load_shares(amount, rows * top, reach, skew, False)
    places = jnp.arange(amount)

    def named(sizes, turn):
        used = int((sizes > 0).sum())
        fixed = max(1, used // 4)
        shifted = fixed + (places - fixed + turn * (used - fixed)) % max(1, amount - fixed)
        return jnp.zeros((amount,), jnp.int32).at[sequence[jnp.where(places < fixed, places, shifted)]].set(jnp.asarray(sizes, jnp.int32))

    sizes = jnp.where(number % 4 == 0, named(packed, number // 4), named(ordinary, number - number // 4 - 1))
    mixed = jax.random.permutation(jax.random.fold_in(own, 3), amount)
    donor, taker = mixed[0:amount // 2 * 2:2], mixed[1:amount // 2 * 2:2]
    room = jnp.minimum(sizes[donor] - 1, reach - sizes[taker]) // 2
    room = jnp.where((donor == sequence[0]) | (taker == sequence[0]) | (sizes[taker] == 0), 0, jnp.maximum(room, 0))
    shifted = jax.random.randint(jax.random.fold_in(own, 4), (amount // 2,), 0, 1 << 20) % (room + 1)
    sizes = sizes.at[donor].add(-shifted).at[taker].add(shifted)
    members = jnp.searchsorted(jnp.cumsum(sizes), jnp.arange(rows * top), side="right").astype(jnp.int32)
    table = members.reshape(top, rows).T
    table = table[jax.random.permutation(jax.random.fold_in(own, 1), rows)]
    turn = jax.random.randint(jax.random.fold_in(own, 2), (rows, 1), 0, top)
    return jnp.take_along_axis(table, (jnp.arange(top)[None, :] + turn) % top, axis=1)


def load_shares(count, total, most, slope, full):
    weights = [(1 << 20) // math.isqrt(standing ** slope) + 1 for standing in range(1, count + 1)]
    largest = most if full else min(most, max(-(-total // count), total * weights[0] // sum(weights)))
    least = 1 if total - largest >= count - 1 else 0
    counts, spare = [largest] + [least] * (count - 1), total - largest - least * (count - 1)
    while spare > 0:
        movable = [i for i in range(1, count) if counts[i] < largest] or [i for i in range(1, count) if counts[i] < most]
        pool, left = sum([weights[i] for i in movable]), spare
        for i in movable:
            addition = min(most - counts[i], max(1, left * weights[i] // pool), spare)
            counts[i] = counts[i] + addition
            spare = spare - addition
    return np.array(counts)


def scatter_about(key, extent, deviation, bound, cuts=(), held_as=jnp.bfloat16):
    result = deviation * jax.random.normal(key, extent, jnp.float32)
    if cuts:
        result = result * level_of(key, extent, cuts, -0.22, 0.18)
    return jnp.clip(result, -bound, bound).astype(held_as)


def setup_inputs(seed: int = 0) -> dict:
    arg_keys = jax.random.split(jax.random.key(seed), 10)
    offsets = jnp.clip(1.0 * jax.random.uniform(arg_keys[0], (3, PARTICLES), jnp.float32) ** level_of(arg_keys[0], (3, PARTICLES), ((1, 32),), -0.2, 0.2), 0.0, 1.0)
    masses = jnp.clip(jnp.exp(math.log(4.0) - 2.7725887 * jax.random.uniform(arg_keys[1], (PARTICLES,), jnp.float32) ** level_of(arg_keys[1], (PARTICLES,), ((0, 32),), -0.2, 0.2)), 0.25, 4.0)
    velocities = scatter_about(arg_keys[2], (3, PARTICLES), 1.0, 5.0, ((1, 32),), jnp.float32)
    destination_keys = jax.random.split(jax.random.fold_in(arg_keys[3], 1), PARTICLES // PART_DEV)
    destination_turns = jax.random.permutation(jax.random.fold_in(arg_keys[3], 3), PARTICLES // PART_DEV)
    destination = jax.vmap(lambda own, number: deal_out(jax.random.fold_in(arg_keys[3], 2), own, number, PART_DEV, DEVICES, 1, CAP, 1))(destination_keys, destination_turns).reshape((PARTICLES, 1))
    first_weight = scatter_about(arg_keys[4], (CH, C_IN, 3, 3, 3), (27 * C_IN) ** -0.5, 0.625)
    first_bias = scatter_about(arg_keys[5], (CH,), 0.5, 3.0, (), jnp.float32)
    second_weight = scatter_about(arg_keys[6], (CH, CH, 3, 3, 3), (27 * CH) ** -0.5, 0.3125)
    second_bias = scatter_about(arg_keys[7], (CH,), 0.5, 3.0, (), jnp.float32)
    cotangent = scatter_about(arg_keys[8], (CH, NY, NZ, NXW), 1.0, 6.0, ((1, 4), (2, 8)))
    return dict(offsets=offsets, masses=masses, velocities=velocities, destination=destination, first_weight=first_weight, first_bias=first_bias, second_weight=second_weight, second_bias=second_bias, cotangent=cotangent)


def cell_split(coord, span):
    position = coord * span
    cell = jnp.minimum(jnp.floor(position).astype(jnp.int32), span - 1)
    frac = position - cell.astype(position.dtype)
    return (cell, frac)

def deposit_cloud(offsets, masses, velocities, base_y, base_z, span_y, span_z, span_x, grid_y, grid_z, grid_x):
    cell_y, frac_y = cell_split(offsets[0], span_y)
    cell_z, frac_z = cell_split(offsets[1], span_z)
    cell_x, frac_x = cell_split(offsets[2], span_x)
    charges = jnp.concatenate([masses[None, :], masses[None, :] * velocities], axis=0)
    total = jnp.zeros((charges.shape[0], grid_y * grid_z * grid_x), masses.dtype)
    for step_y in range(2):
        weight_y = frac_y if step_y else 1.0 - frac_y
        for step_z in range(2):
            weight_z = frac_z if step_z else 1.0 - frac_z
            for step_x in range(2):
                weight_x = frac_x if step_x else 1.0 - frac_x
                index = ((base_y + cell_y + step_y) * grid_z + (base_z + cell_z + step_z)) * grid_x + cell_x + step_x
                total = total.at[:, index].add(charges * (weight_y * weight_z * weight_x)[None, :])
    return total.reshape(charges.shape[0], grid_y, grid_z, grid_x)

def conv_valid(source, kernel):
    return lax.conv_general_dilated(source[None], kernel, (1, 1, 1), 'VALID', dimension_numbers=('NCDHW', 'OIDHW', 'NCDHW'), preferred_element_type=jnp.float32)[0]

def padded32(field):
    return jnp.pad(field.astype(jnp.float32), ((0, 0), (1, 1), (1, 1), (1, 1)))

def flipped(kernel):
    return jnp.flip(kernel, (2, 3, 4)).transpose(1, 0, 2, 3, 4)

def dsilu(value):
    sig = jax.nn.sigmoid(value)
    return sig * (1.0 + value * (1.0 - sig))

def kernel_grad(source, delta, kernel):
    source_pad = padded32(source)
    _, pull = jax.vjp(lambda weights: conv_valid(source_pad, weights), kernel.astype(jnp.float32))
    return pull(delta.astype(jnp.float32))[0]

def reference(offsets, masses, velocities, destination, first_weight, first_bias, second_weight, second_bias, cotangent):
    target = destination[:, 0]
    base_y = target // N_GZ * BY
    base_z = target % N_GZ * BZ
    whole = deposit_cloud(offsets, masses, velocities, base_y, base_z, BY, BZ, NXW, NY + 1, NZ + 1, NXW + 1)
    density = whole[:, :NY, :NZ, :NXW].astype(jnp.bfloat16)
    pre_one = conv_valid(padded32(density), first_weight.astype(jnp.float32)) + first_bias[:, None, None, None]
    active = jax.nn.silu(pre_one).astype(jnp.bfloat16)
    pre_two = conv_valid(padded32(active), second_weight.astype(jnp.float32)) + second_bias[:, None, None, None]
    refined = jax.nn.silu(pre_two).astype(jnp.bfloat16)
    delta_two = (cotangent.astype(jnp.float32) * dsilu(pre_two)).astype(jnp.bfloat16)
    back_one = conv_valid(padded32(delta_two), flipped(second_weight).astype(jnp.float32))
    delta_one = (back_one * dsilu(pre_one)).astype(jnp.bfloat16)
    grad_field = conv_valid(padded32(delta_one), flipped(first_weight).astype(jnp.float32))
    scale = 1.0 / jnp.sqrt(jnp.float32(NY * NZ * NXW))
    grad_second_weight = kernel_grad(active, delta_two, second_weight) * scale
    grad_second_bias = lax.optimization_barrier(jnp.sum(delta_two.astype(jnp.float32), axis=(1, 2, 3))) * scale
    grad_first_weight = kernel_grad(density, delta_one, first_weight) * scale
    grad_first_bias = lax.optimization_barrier(jnp.sum(delta_one.astype(jnp.float32), axis=(1, 2, 3))) * scale
    return (refined, grad_field, grad_first_weight, grad_first_bias, grad_second_weight, grad_second_bias)
```

```python
import functools
import math

import jax
import jax.numpy as jnp
from jax import lax
from jax.experimental import pallas as pl
from jax.experimental.pallas import tpu as pltpu
from jax.sharding import PartitionSpec as P

BF = jnp.bfloat16
F32 = jnp.float32
LANES = 128
VALUES = 10
VMEM_LIMIT = 48 * 1024 * 1024


def _iota(shape, dim):
    return lax.broadcasted_iota(jnp.int32, shape, dim)


def _dot(a, b):
    return jnp.dot(a, b, preferred_element_type=F32)


def _dot_lanes(a, b):
    return lax.dot_general(a, b, (((1,), (1,)), ((), ())), preferred_element_type=F32)


def _call(kernel, out_shape, scratch=(), flops=0, moved=0):
    return pl.pallas_call(
        kernel,
        out_shape=out_shape,
        scratch_shapes=list(scratch),
        compiler_params=pltpu.CompilerParams(vmem_limit_bytes=VMEM_LIMIT),
        cost_estimate=pl.CostEstimate(flops=flops, bytes_accessed=moved, transcendentals=0),
    )


def _route_kernel(devices, spans, off_ref, mass_ref, vel_ref, dest_ref, out_ref, acc_ref, base_ref):
    particles = dest_ref.shape[1]
    capacity = 2 * particles // devices
    pieces = capacity // LANES
    width = 512
    lo_count = 2 * LANES
    hi_count = 2 * particles // lo_count
    acc_ref[...] = jnp.zeros_like(acc_ref)
    base_ref[...] = jnp.zeros_like(base_ref)
    row, col = _iota((LANES, 2 * LANES), 0), _iota((LANES, 2 * LANES), 1)
    prefix = jnp.where((row <= col) | (col >= LANES), 1.0, 0.0).astype(BF)

    def step(i, carry):
        lanes = pl.ds(pl.multiple_of(i * width, width), width)
        dest = dest_ref[:, lanes]
        chosen = jnp.where(_iota((devices, width), 0) == dest, 1.0, 0.0)
        base = base_ref[...]
        ranks = []
        for j in range(width // LANES):
            mine = chosen[:, j * LANES : (j + 1) * LANES]
            counts = _dot(mine.astype(BF), prefix)
            ranks.append(jnp.sum(mine * (counts[:, :LANES] + base), axis=0, keepdims=True))
            base = base + counts[:, LANES:]
        base_ref[...] = base
        rank = jnp.concatenate(ranks, axis=1).astype(jnp.int32) - 1
        if pieces >= 2:
            hi = (rank >> 8) * devices + dest
            lo = rank & 255
        else:
            half = devices // 2
            upper = dest >= half
            hi = jnp.where(upper, dest - half, dest)
            lo = rank + jnp.where(upper, LANES, 0)
        rows = []
        for axis in range(3):
            position = off_ref[axis : axis + 1, lanes] * spans[axis]
            coarse = position.astype(BF)
            rows.append(coarse)
            rows.append((position - coarse.astype(F32)).astype(BF))
        mass = mass_ref[:, lanes]
        rows.append(mass.astype(BF))
        for axis in range(3):
            rows.append((mass * vel_ref[axis : axis + 1, lanes]).astype(BF))
        at_hi = jnp.where(_iota((hi_count, width), 0) == hi, 1.0, 0.0).astype(BF)
        at_lo = jnp.where(_iota((lo_count, width), 0) == lo, 1.0, 0.0).astype(BF)
        spread = jnp.concatenate([at_hi * value for value in rows], axis=0)
        acc_ref[...] += _dot_lanes(spread, at_lo)
        return carry

    lax.fori_loop(0, particles // width, step, 0)
    halves = []
    for half in range(2):
        part = acc_ref[:, half * LANES : (half + 1) * LANES]
        if pieces >= 2:
            halves.append(part.reshape(VALUES * pieces // 2, devices, LANES))
        else:
            halves.append(part.reshape(VALUES, devices // 2, LANES))
    whole = jnp.concatenate(halves, axis=0 if pieces >= 2 else 1)
    out_ref[...] = jnp.transpose(whole, (1, 0, 2)).astype(BF)


def _route(offsets, masses, velocities, destination, devices, spans):
    particles = masses.shape[0]
    capacity = 2 * particles // devices
    rows = VALUES * capacity // LANES
    return _call(
        functools.partial(_route_kernel, devices, spans),
        jax.ShapeDtypeStruct((devices, rows, LANES), BF),
        [
            pltpu.VMEM((VALUES * 2 * particles // 256, 256), F32),
            pltpu.VMEM((devices, LANES), F32),
        ],
        flops=4_000_000_000,
        moved=1_000_000,
    )(offsets, masses.reshape(1, particles), velocities, destination.reshape(1, particles))


def _deposit_kernel(span_y, arrived_ref, cot_ref, own_ref, next_ref, prev_ref, acc_ref):
    sources, height, _ = arrived_ref.shape
    pieces = height // VALUES
    group = max(1, 4 // pieces)
    width = group * pieces * LANES
    span_x = LANES
    acc_ref[...] = jnp.zeros_like(acc_ref)

    def value_rows(blocks, value):
        parts = []
        for block in blocks:
            for piece in range(pieces):
                if pieces >= 2:
                    half = pieces // 2
                    at = (piece % 2) * VALUES * half + value * half + piece // 2
                else:
                    at = value
                parts.append(block[at : at + 1, :])
        return jnp.concatenate(parts, axis=1)

    def step(i, carry):
        blocks = [arrived_ref[i * group + g].astype(F32) for g in range(group)]
        pos_y = value_rows(blocks, 0) + value_rows(blocks, 1)
        pos_z = value_rows(blocks, 2) + value_rows(blocks, 3)
        pos_x = value_rows(blocks, 4) + value_rows(blocks, 5)
        charges = jnp.concatenate([value_rows(blocks, 6 + c) for c in range(4)] * 2, axis=0)
        cell_x = _iota((span_x, width), 0).astype(F32)
        hat_x = jnp.maximum(1.0 - jnp.abs(cell_x - pos_x), 0.0).astype(BF)
        cell_z = (_iota((40, width), 0) >> 2).astype(F32)
        hat_z = jnp.maximum(1.0 - jnp.abs(cell_z - pos_z), 0.0)
        planes = hat_z * jnp.concatenate([charges] * 5, axis=0)
        shares = [
            planes * jnp.maximum(1.0 - jnp.abs(y - pos_y), 0.0) for y in range(span_y + 1)
        ]
        acc_ref[...] += _dot_lanes(jnp.concatenate(shares, axis=0).astype(BF), hat_x)
        return carry

    lax.fori_loop(0, sources // group, step, 0)
    own = jnp.concatenate([acc_ref[y * 40 : (y + 1) * 40, :] for y in range(span_y + 1)], axis=1)
    own_ref[...] = own
    lanes = own.shape[1]
    next_ref[0:32, :] = jnp.concatenate([own[16:40], jnp.zeros((8, lanes), F32)], axis=0).astype(BF)
    next_ref[32:64, 0 : lanes - LANES] = cot_ref[96:128, :]
    next_ref[32:64, lanes - LANES :] = jnp.zeros((32, LANES), BF)
    prev_ref[0:16, :] = own[0:16].astype(BF)
    prev_ref[16:48, 0 : lanes - LANES] = cot_ref[0:32, :]
    prev_ref[16:48, lanes - LANES :] = jnp.zeros((32, LANES), BF)


def _turn_kernel(cot_ref, out_ref):
    channels, span_y, span_z, _ = cot_ref.shape
    size = channels * span_z
    strips = [
        jnp.concatenate([cot_ref[o, y].astype(F32) for o in range(channels)], axis=0)
        for y in range(span_y)
    ]
    field = jnp.concatenate(strips, axis=1).astype(BF)
    row, col = _iota((size, size), 0), _iota((size, size), 1)
    order = (row % channels) * span_z + row // channels
    out_ref[...] = _dot(jnp.where(col == order, 1.0, 0.0).astype(BF), field).astype(BF)


def _merge_kernel(count_z, own_ref, cot_ref, left_ref, right_ref, wide_ref, cotw_ref, first_ref, second_ref):
    keep = jnp.where(lax.axis_index("gz") < count_z - 1, 1.0, 0.0)
    even = lax.axis_index("gy") % 2 == 0
    left = left_ref[0:32, :].astype(F32)
    right = right_ref[0:16, :].astype(F32)
    own = own_ref[...]
    wide = jnp.concatenate(
        [
            left[0:16],
            own[0:8] + left[16:24],
            own[8:32],
            own[32:40] * keep + right[0:8],
            right[8:16],
        ],
        axis=0,
    )
    wide_ref[...] = wide
    cells = cot_ref.shape[1]
    cotw_ref[0:32, :] = left_ref[32:64, 0:cells]
    cotw_ref[32:160, :] = cot_ref[...]
    cotw_ref[160:192, :] = right_ref[16:48, 0:cells]

    def to_next(out):
        out[:, 0:640] = wide[:, 512:1152].astype(BF)
        for i in range(3):
            out[:, 640 + 256 * i : 896 + 256 * i] = cotw_ref[64 * i : 64 * (i + 1), cells - 256 : cells]

    def to_prev(out):
        out[:, 0:512] = wide[:, 0:512].astype(BF)
        out[:, 512:640] = jnp.zeros((64, 128), BF)
        for i in range(3):
            out[:, 640 + 256 * i : 896 + 256 * i] = cotw_ref[64 * i : 64 * (i + 1), 0:256]

    @pl.when(even)
    def _():
        to_next(first_ref)
        to_prev(second_ref)

    @pl.when(jnp.logical_not(even))
    def _():
        to_prev(first_ref)
        to_next(second_ref)


def _weights_kernel(k1_ref, k2_ref, w1_ref, w2_ref, wb_ref, wf_ref, scr_ref):
    def wide(x):
        rows, cols = x.shape
        return jnp.concatenate([x, jnp.zeros((rows, LANES - cols), F32)], axis=1)

    def base(block, stride, step, total):
        out = None
        for tx in range(3):
            for tz in range(3):
                x = wide(block(tz, tx))
                x = jnp.concatenate([x, jnp.zeros((x.shape[0], total - LANES), F32)], axis=1)
                at = tx * stride + tz * step
                x = pltpu.roll(x, at, 1) if at else x
                out = x if out is None else out + x
        return out

    for ty in range(3):
        def tap(tz, tx):
            return (ty * 3 + tz) * 3 + tx

        def back(tz, tx):
            return 26 - tap(tz, tx)

        b = base(lambda tz, tx: jnp.swapaxes(wide(k1_ref[tap(tz, tx)].astype(F32)), 0, 1)[0:16, :], 64, 4, 256)
        for z in range(14):
            w1_ref[ty, z * 16 : (z + 1) * 16, :] = (pltpu.roll(b, 4 * z, 1) if z else b).astype(BF)
        b = base(lambda tz, tx: k2_ref[tap(tz, tx)].astype(F32), 256, 16, 768)
        for z in range(12):
            w2_ref[ty, z * 16 : (z + 1) * 16, :] = (pltpu.roll(b, 16 * z, 1) if z else b).astype(BF)
        b = base(lambda tz, tx: jnp.swapaxes(wide(k2_ref[back(tz, tx)].astype(F32)), 0, 1)[0:16, :], 192, 16, 640)
        for z in range(10):
            wb_ref[ty, z * 16 : (z + 1) * 16, :] = (pltpu.roll(b, 16 * z, 1) if z else b).astype(BF)
        b = base(lambda tz, tx: k1_ref[back(tz, tx)].astype(F32), 160, 16, 512)
        for z in range(8):
            moved = pltpu.roll(b, 16 * z, 1) if z else b
            for c in range(4):
                scr_ref[c * 8 + z : c * 8 + z + 1, :] = moved[c : c + 1, :]
        wf_ref[ty] = scr_ref[...].astype(BF)


def _net_kernel(
    count_y, count_z, wide_ref, cotw_ref, ra_ref, rb_ref, w1_ref, w2_ref, wb_ref, wf_ref,
    b1_ref, b2_ref, refined_ref, field_ref, sums_ref,
    msg_ref, dens_ref, act_ref, del_ref, one_ref, ds_ref, ref_ref,
):
    me_y, me_z = lax.axis_index("gy"), lax.axis_index("gz")
    even = me_y % 2 == 0

    @pl.when(even)
    def _():
        msg_ref[0] = rb_ref[...]
        msg_ref[1] = ra_ref[...]

    @pl.when(jnp.logical_not(even))
    def _():
        msg_ref[0] = ra_ref[...]
        msg_ref[1] = rb_ref[...]

    edge = _iota((1, LANES), 1)
    first_lane, last_lane = edge == 0, edge == LANES - 1

    def shifted(value, dst, row0, stride, lane0):
        rows, lanes = value.shape
        for y in range(lanes // LANES):
            block = value[:, y * LANES : (y + 1) * LANES]
            at = slice(lane0 + y * LANES, lane0 + (y + 1) * LANES)
            left = jnp.where(first_lane, 0.0, pltpu.roll(block, 1, 1))
            right = jnp.where(last_lane, 0.0, pltpu.roll(block, LANES - 1, 1))
            dst[row0 : row0 + rows, at] = left.astype(BF)
            dst[row0 + stride : row0 + stride + rows, at] = block.astype(BF)
            dst[row0 + 2 * stride : row0 + 2 * stride + rows, at] = right.astype(BF)

    keep_y = jnp.where(me_y < count_y - 1, 1.0, 0.0)
    up = msg_ref[0, :, 0:640].astype(F32)
    down = msg_ref[1, :, 0:512].astype(F32)
    shifted(up[:, 0:512], dens_ref, 0, 64, 0)
    shifted(wide_ref[:, 0:128] + up[:, 512:640], dens_ref, 0, 64, 512)
    shifted(wide_ref[:, 128:1024], dens_ref, 0, 64, 640)
    shifted(wide_ref[:, 1024:1152] * keep_y + down[:, 0:128], dens_ref, 0, 64, 1536)
    shifted(down[:, 128:512], dens_ref, 0, 64, 1664)

    eye = _iota((16, 16), 0) == _iota((16, 16), 1)

    def column(bias_ref, count):
        one = jnp.sum(jnp.where(eye, bias_ref[...], 0.0), axis=1, keepdims=True)
        return jnp.concatenate([one] * count, axis=0)

    def inside_z(rows, halo):
        z = me_z * 8 - halo + (_iota((rows, 1), 0) >> 4)
        return jnp.where((z >= 0) & (z < count_z * 8), 1.0, 0.0)

    def inside_y(first, halo):
        y = me_y * 8 - halo + first + (_iota((1, 256), 1) >> 7)
        return jnp.where((y >= 0) & (y < count_y * 8), 1.0, 0.0)

    bias = column(b1_ref, 14)
    mask_z = inside_z(224, 3)
    for tx in range(3):
        act_ref[tx * 256 + 224 : (tx + 1) * 256, :] = jnp.zeros((32, act_ref.shape[1]), BF)
    for n in range(7):
        pre = bias
        for ty in range(3):
            at = (2 * n + ty) * LANES
            pre = pre + _dot(w1_ref[ty, :, 0:192], dens_ref[:, at : at + 256])
        sig = 0.5 * jnp.tanh(0.5 * pre) + 0.5
        act = pre * sig
        if 1 <= n <= 5:
            mid = slice(32, 192)
            ds_ref[:, (n - 1) * 256 : n * 256] = sig[mid] * (1.0 + pre[mid] - act[mid])
        shifted(act * (mask_z * inside_y(2 * n, 3)), act_ref, 0, 256, n * 256)

    bias = column(b2_ref, 12)
    for n in range(6):
        pre = bias
        for ty in range(3):
            at = (2 * n + ty) * LANES
            pre = pre + _dot(w2_ref[ty], act_ref[:, at : at + 256])
        sig = 0.5 * jnp.tanh(0.5 * pre) + 0.5
        act = pre * sig
        if n == 0 or n == 5:
            side = 0 if n == 0 else 1
            cot = jnp.concatenate(
                [msg_ref[side, :, 640 + 256 * i : 896 + 256 * i] for i in range(3)], axis=0
            )
        else:
            cot = cotw_ref[:, (n - 1) * 256 : n * 256]
            ref_ref[:, (n - 1) * 256 : n * 256] = act[32:160].astype(BF)
        shifted(cot.astype(F32) * (sig * (1.0 + pre - act)), del_ref, 0, 192, n * 256)

    mask_z = inside_z(160, 1)
    for n in range(5):
        back = None
        for ty in range(3):
            at = (2 * n + ty) * LANES
            term = _dot(wb_ref[ty, :, 0:576], del_ref[:, at : at + 256])
            back = term if back is None else back + term
        back = back * ds_ref[:, n * 256 : (n + 1) * 256] * (mask_z * inside_y(2 * n, 1))
        shifted(back, one_ref, 0, 160, n * 256)

    for n in range(4):
        grad = None
        for ty in range(3):
            at = (2 * n + ty) * LANES
            term = _dot(wf_ref[ty, :, 0:480], one_ref[:, at : at + 256])
            grad = term if grad is None else grad + term
        for y in range(2):
            for c in range(4):
                field_ref[c, 2 * n + y] = grad[c * 8 : (c + 1) * 8, y * LANES : (y + 1) * LANES]

    row, col = _iota((128, 128), 0), _iota((128, 128), 1)
    order = jnp.where(col == (row % 8) * 16 + row // 8, 1.0, 0.0).astype(BF)
    for n in range(4):
        turned = _dot(order, ref_ref[:, n * 256 : (n + 1) * 256]).astype(BF)
        for y in range(2):
            for o in range(16):
                refined_ref[o, 2 * n + y] = turned[o * 8 : (o + 1) * 8, y * LANES : (y + 1) * LANES]

    lane_z = _iota((1, LANES), 1) >> 4
    own_two = del_ref[224:352, 256:1280]
    own_one = one_ref[176:304, 128:1152]

    def folded(value):
        for step in (64, 32, 16):
            value = value + pltpu.roll(value, step, 1)
        return value

    def packed(taps, rows):
        groups = []
        for g in range(4):
            out = jnp.zeros((rows, LANES), F32)
            for t in range(8 * g, min(8 * g + 8, len(taps))):
                out = jnp.where(lane_z == t % 8, taps[t], out)
            groups.append(out)
        return groups

    taps = [None] * 27
    for ty in range(3):
        for tx in range(3):
            lanes = slice((2 + ty) * LANES, (2 + ty) * LANES + 1024)
            pairs = _dot_lanes(act_ref[tx * 256 + 32 : tx * 256 + 192, lanes], own_two)
            for tz in range(3):
                total = jnp.zeros((16, LANES), F32)
                for z in range(tz, tz + 8):
                    total = total + jnp.where(lane_z == z - tz, pairs[z * 16 : (z + 1) * 16], 0.0)
                taps[(ty * 3 + tz) * 3 + tx] = folded(total)
    ones = jnp.ones((16, 1024), BF)
    taps.append(folded(_dot_lanes(ones, own_two)))
    taps.append(folded(_dot_lanes(ones, own_one)))
    for g, group in enumerate(packed(taps, 16)):
        sums_ref[g * 16 : (g + 1) * 16, :] = group

    taps = [None] * 27
    row_z = (_iota((64, LANES), 0) >> 2) - (_iota((64, LANES), 1) >> 4) - 3
    for ty in range(3):
        for tx in range(3):
            lanes = slice((3 + ty) * LANES, (3 + ty) * LANES + 1024)
            pairs = _dot_lanes(dens_ref[tx * 64 : (tx + 1) * 64, lanes], own_one)
            for tz in range(3):
                chosen = jnp.where(row_z == tz, pairs, 0.0)
                total = chosen[0:8]
                for i in range(1, 8):
                    total = total + chosen[i * 8 : (i + 1) * 8]
                total = total + pltpu.roll(total, 4, 0)
                taps[(ty * 3 + tz) * 3 + tx] = folded(total)
    upper = _iota((8, LANES), 0) < 4
    groups = packed(taps, 8)
    sums_ref[64:72, :] = jnp.where(upper, groups[0], groups[1])
    sums_ref[72:80, :] = jnp.where(upper, groups[2], groups[3])


def _finish_kernel(scale, a_ref, b_ref, c_ref, d_ref, k1_ref, b1_ref, k2_ref, b2_ref):
    total = ((a_ref[...] + b_ref[...]) + (c_ref[...] + d_ref[...])) * scale
    for g in range(4):
        block = jnp.swapaxes(total[g * 16 : (g + 1) * 16, :], 0, 1)
        for j in range(8):
            t = g * 8 + j
            if t < 27:
                k2_ref[t] = block[j * 16 : (j + 1) * 16, :]
    tail = total[48:49, :]
    b2_ref[...] = tail[:, 48:64]
    b1_ref[...] = tail[:, 64:80]
    for t in range(27):
        g = t // 8
        rows = 64 + 8 * (g // 2) + 4 * (g % 2)
        k1_ref[t] = total[rows : rows + 4, (t % 8) * 16 : (t % 8) * 16 + 16]


def _local(
    offsets,
    masses,
    velocities,
    destination,
    first_weight,
    first_bias,
    second_weight,
    second_bias,
    cotangent,
):
    count_y = lax.axis_size("gy")
    count_z = lax.axis_size("gz")
    devices = count_y * count_z
    channels, span_y, span_z, span_x = cotangent.shape
    spans = (float(span_y), float(span_z), float(span_x))
    lanes = span_y * span_x
    both = ("gy", "gz")

    outgoing = _route(offsets, masses, velocities, destination, devices, spans)
    arrived = lax.all_to_all(outgoing, both, split_axis=0, concat_axis=0, tiled=True)

    turned = _call(
        _turn_kernel, jax.ShapeDtypeStruct((channels * span_z, lanes), BF), flops=10**8, moved=10**6
    )(cotangent)
    own, to_next, to_prev = _call(
        functools.partial(_deposit_kernel, span_y),
        (
            jax.ShapeDtypeStruct((40, lanes + span_x), F32),
            jax.ShapeDtypeStruct((64, lanes + span_x), BF),
            jax.ShapeDtypeStruct((48, lanes + span_x), BF),
        ),
        [pltpu.VMEM((40 * (span_y + 1), span_x), F32)],
        flops=4 * 10**9,
        moved=10**6,
    )(arrived, turned)
    left = lax.ppermute(to_next, "gz", [(i, i + 1) for i in range(count_z - 1)])
    right = lax.ppermute(to_prev, "gz", [(i + 1, i) for i in range(count_z - 1)])
    k1 = first_weight.transpose(2, 3, 4, 1, 0).reshape(27, 4, 16)
    k2 = second_weight.transpose(2, 3, 4, 0, 1).reshape(27, 16, 16)
    banded = _call(
        _weights_kernel,
        (
            jax.ShapeDtypeStruct((3, 224, 256), BF),
            jax.ShapeDtypeStruct((3, 192, 768), BF),
            jax.ShapeDtypeStruct((3, 160, 640), BF),
            jax.ShapeDtypeStruct((3, 32, 512), BF),
        ),
        [pltpu.VMEM((32, 512), F32)],
        flops=2 * 10**9,
        moved=2 * 10**6,
    )(k1, k2)
    wide, cot_wide, first, second = _call(
        functools.partial(_merge_kernel, count_z),
        (
            jax.ShapeDtypeStruct((64, lanes + span_x), F32),
            jax.ShapeDtypeStruct((192, lanes), BF),
            jax.ShapeDtypeStruct((64, 1408), BF),
            jax.ShapeDtypeStruct((64, 1408), BF),
        ),
        flops=10**6,
        moved=10**6,
    )(own, turned, left, right)
    inner = [(i, i ^ 1) for i in range(count_y)]
    outer = [(i, i + 1) for i in range(1, count_y - 1, 2)]
    outer = outer + [(j, i) for i, j in outer]
    got_first = lax.ppermute(first, "gy", inner)
    got_second = lax.ppermute(second, "gy", outer)
    refined, grad_field, sums = _call(
        functools.partial(_net_kernel, count_y, count_z),
        (
            jax.ShapeDtypeStruct(cotangent.shape, BF),
            jax.ShapeDtypeStruct((4,) + cotangent.shape[1:], F32),
            jax.ShapeDtypeStruct((80, LANES), F32),
        ),
        [
            pltpu.VMEM((2, 64, 1408), BF),
            pltpu.VMEM((192, 2048), BF),
            pltpu.VMEM((768, 1792), BF),
            pltpu.VMEM((576, 1536), BF),
            pltpu.VMEM((480, 1280), BF),
            pltpu.VMEM((160, 1280), F32),
            pltpu.VMEM((128, 1024), BF),
        ],
        flops=6 * 10**9,
        moved=2 * 10**6,
    )(
        wide, cot_wide, got_first, got_second, *banded,
        first_bias.reshape(1, 16), second_bias.reshape(1, 16),
    )

    def swapped(value, bit):
        return lax.ppermute(value, both, [(i, i ^ bit) for i in range(devices)])

    bits = [1 << i for i in range((devices - 1).bit_length())]
    inner_bit = count_z
    rest = [b for b in bits if b != inner_bit]
    total = sums + swapped(sums, inner_bit)
    while len(rest) > 2:
        a = rest.pop()
        if len(rest) > 2:
            b = rest.pop(0)
            total = (total + swapped(total, a)) + (swapped(total, b) + swapped(total, a ^ b))
        else:
            total = total + swapped(total, a)
    a, b = rest
    parts = (total, swapped(total, a), swapped(total, b), swapped(total, a ^ b))
    scale = 1.0 / math.sqrt(span_y * span_z * span_x * devices)
    g1, gb1, g2, gb2 = _call(
        functools.partial(_finish_kernel, scale),
        (
            jax.ShapeDtypeStruct((27, 4, 16), F32),
            jax.ShapeDtypeStruct((1, 16), F32),
            jax.ShapeDtypeStruct((27, 16, 16), F32),
            jax.ShapeDtypeStruct((1, 16), F32),
        ),
        flops=10**5,
        moved=10**5,
    )(*parts)
    return (
        refined,
        grad_field,
        g1.reshape(3, 3, 3, 4, 16).transpose(4, 3, 0, 1, 2),
        gb1.reshape(16),
        g2.reshape(3, 3, 3, 16, 16).transpose(3, 4, 0, 1, 2),
        gb2.reshape(16),
    )


def solution(mesh):
    placed = (
        P(None, ("gy", "gz")),
        P(("gy", "gz")),
        P(None, ("gy", "gz")),
        P(("gy", "gz"), None),
        P(),
        P(),
        P(),
        P(),
        P(None, "gy", "gz", None),
    )
    return jax.shard_map(
        _local,
        mesh=mesh,
        in_specs=placed,
        out_specs=(P(None, "gy", "gz", None), P(None, "gy", "gz", None), P(), P(), P(), P()),
        check_vma=False,
    )
```

```python
import functools
import math

import jax
import jax.numpy as jnp
from jax import lax
from jax.experimental import pallas as pl
from jax.experimental.pallas import tpu as pltpu
from jax.sharding import PartitionSpec as P

BF = jnp.bfloat16
F32 = jnp.float32
LANES = 128
VALUES = 10
VMEM_LIMIT = 48 * 1024 * 1024
ROUTE_VMEM_LIMIT = 60 * 1024 * 1024
ROUTE_WIDTH = 512


def _iota(shape, dim):
    return lax.broadcasted_iota(jnp.int32, shape, dim)


def _dot(a, b):
    return jnp.dot(a, b, preferred_element_type=F32)


def _dot_lanes(a, b):
    return lax.dot_general(a, b, (((1,), (1,)), ((), ())), preferred_element_type=F32)


def _call(kernel, out_shape, scratch=(), flops=0, moved=0):
    return pl.pallas_call(
        kernel,
        out_shape=out_shape,
        scratch_shapes=list(scratch),
        compiler_params=pltpu.CompilerParams(vmem_limit_bytes=VMEM_LIMIT),
        cost_estimate=pl.CostEstimate(flops=flops, bytes_accessed=moved, transcendentals=0),
    )


def _route_kernel(
    devices, spans, off_hbm, mass_hbm, vel_hbm, dest_hbm, out_ref,
    off_ref, mass_ref, vel_ref, dest_ref, acc_ref, rank_ref, sems,
):
    loads = [
        pltpu.make_async_copy(src, dst, sems.at[i])
        for i, (src, dst) in enumerate(
            ((dest_hbm, dest_ref), (off_hbm, off_ref), (mass_hbm, mass_ref), (vel_hbm, vel_ref))
        )
    ]
    for load in loads:
        load.start()
    particles = dest_ref.shape[1]
    capacity = 2 * particles // devices
    pieces = capacity // LANES
    width = ROUTE_WIDTH
    lo_count = 2 * LANES
    hi_count = 2 * particles // lo_count
    row, col = _iota((LANES, 2 * LANES), 0), _iota((LANES, 2 * LANES), 1)
    prefix = jnp.where((row <= col) | (col >= LANES), 1.0, 0.0).astype(BF)
    number = _iota((devices, LANES), 0)
    loads[0].wait()

    def count(i, base):
        dests = [
            dest_ref[:, pl.ds(pl.multiple_of((i * 16 + j) * LANES, LANES), LANES)] for j in range(16)
        ]
        chosen = [jnp.where(number == dest, 1.0, 0.0) for dest in dests]
        counts = _dot(jnp.concatenate(chosen, axis=0).astype(BF), prefix)
        for j in range(16):
            mine = counts[j * devices : (j + 1) * devices]
            rank = jnp.sum(chosen[j] * (mine[:, :LANES] + base), axis=0, keepdims=True)
            at = pl.ds(pl.multiple_of((i * 16 + j) * LANES, LANES), LANES)
            rank_ref[:, at] = rank.astype(jnp.int32) - 1
            base = base + mine[:, LANES:]
        return base

    lax.fori_loop(0, particles // (16 * LANES), count, jnp.zeros((devices, LANES), F32), unroll=True)
    for load in loads[1:]:
        load.wait()

    def step(i, carry):
        lanes = slice(i * width, (i + 1) * width)
        dest = dest_ref[:, lanes]
        rank = rank_ref[:, lanes]
        if pieces >= 2:
            hi = (rank >> 8) * devices + dest
            lo = rank & 255
        else:
            half = devices // 2
            upper = dest >= half
            hi = jnp.where(upper, dest - half, dest)
            lo = rank + jnp.where(upper, LANES, 0)
        rows = []
        for axis in range(3):
            position = off_ref[axis : axis + 1, lanes] * spans[axis]
            coarse = position.astype(BF)
            rows.append(coarse)
            rows.append((position - coarse.astype(F32)).astype(BF))
        mass = mass_ref[:, lanes]
        rows.append(mass.astype(BF))
        for axis in range(3):
            rows.append((mass * vel_ref[axis : axis + 1, lanes]).astype(BF))
        at_hi = jnp.where(_iota((hi_count, width), 0) == hi, 1.0, 0.0).astype(BF)
        at_lo = jnp.where(_iota((lo_count, width), 0) == lo, 1.0, 0.0).astype(BF)
        spread = jnp.concatenate([at_hi * value for value in rows], axis=0)
        term = _dot_lanes(spread, at_lo)
        if i == 0:
            acc_ref[...] = term
        else:
            acc_ref[...] += term

    for i in range(particles // width):
        step(i, 0)
    halves = []
    for half in range(2):
        part = acc_ref[:, half * LANES : (half + 1) * LANES]
        if pieces >= 2:
            halves.append(part.reshape(VALUES * pieces // 2, devices, LANES))
        else:
            halves.append(part.reshape(VALUES, devices // 2, LANES))
    whole = jnp.concatenate(halves, axis=0 if pieces >= 2 else 1)
    out_ref[...] = jnp.transpose(whole, (1, 0, 2)).astype(BF)


def _route(offsets, masses, velocities, destination, devices, spans):
    particles = masses.shape[0]
    capacity = 2 * particles // devices
    rows = VALUES * capacity // LANES
    return pl.pallas_call(
        functools.partial(_route_kernel, devices, spans),
        out_shape=jax.ShapeDtypeStruct((devices, rows, LANES), BF),
        in_specs=[pl.BlockSpec(memory_space=pltpu.HBM)] * 4,
        scratch_shapes=[
            pltpu.VMEM((3, particles), F32),
            pltpu.VMEM((1, particles), F32),
            pltpu.VMEM((3, particles), F32),
            pltpu.VMEM((1, particles), jnp.int32),
            pltpu.VMEM((VALUES * 2 * particles // 256, 256), F32),
            pltpu.VMEM((1, particles), jnp.int32),
            pltpu.SemaphoreType.DMA((4,)),
        ],
        compiler_params=pltpu.CompilerParams(vmem_limit_bytes=ROUTE_VMEM_LIMIT),
        cost_estimate=pl.CostEstimate(flops=4 * 10**9, bytes_accessed=10**6, transcendentals=0),
    )(offsets, masses.reshape(1, particles), velocities, destination.reshape(1, particles))


def _deposit_kernel(span_y, arrived_ref, *refs):
    own_ref, first_ref, second_ref, acc_ref = refs[-4:]
    sources, height, _ = arrived_ref.shape
    pieces = height // VALUES
    group = max(1, 4 // pieces)
    width = group * pieces * LANES
    span_x = LANES
    acc_ref[...] = jnp.zeros_like(acc_ref)

    def value_rows(blocks, value):
        parts = []
        for block in blocks:
            for piece in range(pieces):
                if pieces >= 2:
                    half = pieces // 2
                    at = (piece % 2) * VALUES * half + value * half + piece // 2
                else:
                    at = value
                parts.append(block[at : at + 1, :])
        return jnp.concatenate(parts, axis=1)

    def step(i, carry):
        blocks = [arrived_ref[i * group + g].astype(F32) for g in range(group)]
        pos_y = value_rows(blocks, 0) + value_rows(blocks, 1)
        pos_z = value_rows(blocks, 2) + value_rows(blocks, 3)
        pos_x = value_rows(blocks, 4) + value_rows(blocks, 5)
        charges = jnp.concatenate([value_rows(blocks, 6 + c) for c in range(4)] * 2, axis=0)
        cell_x = _iota((span_x, width), 0).astype(F32)
        hat_x = jnp.maximum(1.0 - jnp.abs(cell_x - pos_x), 0.0).astype(BF)
        cell_z = (_iota((40, width), 0) >> 2).astype(F32)
        hat_z = jnp.maximum(1.0 - jnp.abs(cell_z - pos_z), 0.0)
        planes = hat_z * jnp.concatenate([charges] * 5, axis=0)
        cell_y = _iota((16, width), 0).astype(F32)
        hat_y = jnp.maximum(1.0 - jnp.abs(cell_y - pos_y), 0.0)
        shares = [planes * hat_y[y : y + 1] for y in range(span_y + 1)]
        acc_ref[...] += _dot_lanes(jnp.concatenate(shares, axis=0).astype(BF), hat_x)
        return carry

    lax.fori_loop(0, sources // group, step, 0, unroll=True)
    own = jnp.concatenate([acc_ref[y * 40 : (y + 1) * 40, :] for y in range(span_y + 1)], axis=1)
    own_ref[...] = own
    even = lax.axis_index("gz") % 2 == 0
    first_ref[...] = jnp.where(even, own[16:40], own[0:24]).astype(BF)
    second_ref[...] = jnp.where(even, own[0:24], own[16:40]).astype(BF)


def _merge_kernel(count_z, own_ref, fb_ref, fa_ref, wide_ref, first_ref, second_ref):
    keep = jnp.where(lax.axis_index("gz") < count_z - 1, 1.0, 0.0)
    even = lax.axis_index("gy") % 2 == 0
    even_z = lax.axis_index("gz") % 2 == 0
    first, second = fa_ref[...].astype(F32), fb_ref[...].astype(F32)
    left = jnp.where(even_z, second, first)
    right = jnp.where(even_z, first, second)
    own = own_ref[...]
    wide = jnp.concatenate(
        [
            left[0:16],
            own[0:8] + left[16:24],
            own[8:32],
            own[32:40] * keep + right[0:8],
            right[8:16],
        ],
        axis=0,
    )
    wide_ref[...] = wide
    to_next = wide[:, 512:1152]
    to_prev = wide[:, 0:640]
    first_ref[...] = jnp.where(even, to_next, to_prev).astype(BF)
    second_ref[...] = jnp.where(even, to_prev, to_next).astype(BF)


def _turn_kernel(cot_ref, out_ref, first_ref, second_ref):
    channels, span_y, span_z, _ = cot_ref.shape
    size = channels * span_z
    strips = [
        jnp.concatenate([cot_ref[o, y].astype(F32) for o in range(channels)], axis=0)
        for y in range(span_y)
    ]
    field = jnp.concatenate(strips, axis=1).astype(BF)
    row, col = _iota((size, size), 0), _iota((size, size), 1)
    order = (row % channels) * span_z + row // channels
    turned = _dot(jnp.where(col == order, 1.0, 0.0).astype(BF), field)
    out_ref[...] = turned.astype(BF)
    even = lax.axis_index("gz") % 2 == 0
    to_next, to_prev = turned[size - 32 :], turned[0:32]
    first_ref[...] = jnp.where(even, to_next, to_prev).astype(BF)
    second_ref[...] = jnp.where(even, to_prev, to_next).astype(BF)


def _rim_kernel(cot_ref, fb_ref, fa_ref, wide_ref, first_ref, second_ref):
    even = lax.axis_index("gy") % 2 == 0
    even_z = lax.axis_index("gz") % 2 == 0
    first, second = fa_ref[...].astype(F32), fb_ref[...].astype(F32)
    wide_ref[0:32, :] = jnp.where(even_z, second, first).astype(BF)
    wide_ref[32:160, :] = cot_ref[...]
    wide_ref[160:192, :] = jnp.where(even_z, first, second).astype(BF)
    cells = wide_ref.shape[1]
    to_next = wide_ref[:, cells - 256 : cells].astype(F32)
    to_prev = wide_ref[:, 0:256].astype(F32)
    first_ref[...] = jnp.where(even, to_next, to_prev).astype(BF)
    second_ref[...] = jnp.where(even, to_prev, to_next).astype(BF)


def _weights_kernel(
    k1_ref, k2_ref, b1_ref, b2_ref, w1_ref, w2_ref, wb_ref, wf_ref, c1_ref, c2_ref, scr_ref
):
    def wide(x):
        rows, cols = x.shape
        return jnp.concatenate([x, jnp.zeros((rows, LANES - cols), F32)], axis=1)

    def base(block, stride, step, total):
        out = None
        for tx in range(3):
            for tz in range(3):
                x = wide(block(tz, tx))
                x = jnp.concatenate([x, jnp.zeros((x.shape[0], total - LANES), F32)], axis=1)
                at = tx * stride + tz * step
                x = pltpu.roll(x, at, 1) if at else x
                out = x if out is None else out + x
        return out

    for ty in range(3):
        def tap(tz, tx):
            return (ty * 3 + tz) * 3 + tx

        def back(tz, tx):
            return 26 - tap(tz, tx)

        b = base(lambda tz, tx: jnp.swapaxes(wide(k1_ref[tap(tz, tx)].astype(F32)), 0, 1)[0:16, :], 64, 4, 256)
        for z in range(14):
            w1_ref[ty, z * 16 : (z + 1) * 16, :] = (pltpu.roll(b, 4 * z, 1) if z else b).astype(BF)
        b = base(lambda tz, tx: k2_ref[tap(tz, tx)].astype(F32), 256, 16, 768)
        for z in range(12):
            w2_ref[ty, z * 16 : (z + 1) * 16, :] = (pltpu.roll(b, 16 * z, 1) if z else b).astype(BF)
        b = base(lambda tz, tx: jnp.swapaxes(wide(k2_ref[back(tz, tx)].astype(F32)), 0, 1)[0:16, :], 192, 16, 640)
        for z in range(10):
            wb_ref[ty, z * 16 : (z + 1) * 16, :] = (pltpu.roll(b, 16 * z, 1) if z else b).astype(BF)
        b = base(lambda tz, tx: k1_ref[back(tz, tx)].astype(F32), 160, 16, 512)
        for z in range(8):
            moved = pltpu.roll(b, 16 * z, 1) if z else b
            for c in range(4):
                scr_ref[c * 8 + z : c * 8 + z + 1, :] = moved[c : c + 1, :]
        wf_ref[ty] = scr_ref[...].astype(BF)

    eye = _iota((16, 16), 0) == _iota((16, 16), 1)
    for bias_ref, out_ref in ((b1_ref, c1_ref), (b2_ref, c2_ref)):
        one = jnp.sum(jnp.where(eye, bias_ref[...], 0.0), axis=1, keepdims=True)
        out_ref[...] = jnp.broadcast_to(one, (16, 256))


def _net_kernel(
    count_y, count_z, wide_ref, cotw_ref, db_ref, da_ref, cb_ref, ca_ref, w1_ref, w2_ref, wb_ref, wf_ref,
    b1_ref, b2_ref, refined_ref, field_ref, sums_ref,
    side_ref, dens_ref, act_ref, del_ref, one_ref, ds_ref, ref_ref,
):
    me_y, me_z = lax.axis_index("gy"), lax.axis_index("gz")
    even = me_y % 2 == 0

    edge = _iota((1, LANES), 1)
    first_lane, last_lane = edge == 0, edge == LANES - 1

    def shifted(value, dst, row0, stride, lane0):
        rows, lanes = value.shape
        for y in range(lanes // LANES):
            block = value[:, y * LANES : (y + 1) * LANES]
            at = slice(lane0 + y * LANES, lane0 + (y + 1) * LANES)
            left = jnp.where(first_lane, 0.0, pltpu.roll(block, 1, 1))
            right = jnp.where(last_lane, 0.0, pltpu.roll(block, LANES - 1, 1))
            dst[row0 : row0 + rows, at] = left.astype(BF)
            dst[row0 + stride : row0 + stride + rows, at] = block.astype(BF)
            dst[row0 + 2 * stride : row0 + 2 * stride + rows, at] = right.astype(BF)

    keep_y = jnp.where(me_y < count_y - 1, 1.0, 0.0)
    first, second = da_ref[...].astype(F32), db_ref[...].astype(F32)
    up = jnp.where(even, second, first)
    down = jnp.where(even, first, second)
    first, second = ca_ref[...].astype(F32), cb_ref[...].astype(F32)
    side_ref[0] = jnp.where(even, second, first)
    side_ref[1] = jnp.where(even, first, second)
    shifted(up[:, 0:512], dens_ref, 0, 64, 0)
    shifted(wide_ref[:, 0:128] + up[:, 512:640], dens_ref, 0, 64, 512)
    shifted(wide_ref[:, 128:1024], dens_ref, 0, 64, 640)
    shifted(wide_ref[:, 1024:1152] * keep_y + down[:, 0:128], dens_ref, 0, 64, 1536)
    shifted(down[:, 128:512], dens_ref, 0, 64, 1664)

    def inside_z(rows, halo):
        z = me_z * 8 - halo + (_iota((rows, 1), 0) >> 4)
        return jnp.where((z >= 0) & (z < count_z * 8), 1.0, 0.0)

    def inside_y(first, halo):
        y = me_y * 8 - halo + first + (_iota((1, 256), 1) >> 7)
        return jnp.where((y >= 0) & (y < count_y * 8), 1.0, 0.0)

    bias = jnp.concatenate([b1_ref[...]] * 14, axis=0)
    mask_z = inside_z(224, 3)
    for tx in range(3):
        act_ref[tx * 256 + 224 : (tx + 1) * 256, :] = jnp.zeros((32, act_ref.shape[1]), BF)
    for n in range(7):
        pre = bias
        for ty in range(3):
            at = (2 * n + ty) * LANES
            pre = pre + _dot(w1_ref[ty, :, 0:192], dens_ref[:, at : at + 256])
        sig = 0.5 * jnp.tanh(0.5 * pre) + 0.5
        act = pre * sig
        if 1 <= n <= 5:
            mid = slice(32, 192)
            ds_ref[:, (n - 1) * 256 : n * 256] = sig[mid] * (1.0 + pre[mid] - act[mid])
        shifted(act * (mask_z * inside_y(2 * n, 3)), act_ref, 0, 256, n * 256)

    bias = jnp.concatenate([b2_ref[...]] * 12, axis=0)
    for n in range(6):
        pre = bias
        for ty in range(3):
            at = (2 * n + ty) * LANES
            pre = pre + _dot(w2_ref[ty], act_ref[:, at : at + 256])
        sig = 0.5 * jnp.tanh(0.5 * pre) + 0.5
        act = pre * sig
        if n == 0 or n == 5:
            cot = side_ref[0 if n == 0 else 1]
        else:
            cot = cotw_ref[:, (n - 1) * 256 : n * 256].astype(F32)
            ref_ref[:, (n - 1) * 256 : n * 256] = act[32:160].astype(BF)
        shifted(cot * (sig * (1.0 + pre - act)), del_ref, 0, 192, n * 256)

    mask_z = inside_z(160, 1)
    for n in range(5):
        back = None
        for ty in range(3):
            at = (2 * n + ty) * LANES
            term = _dot(wb_ref[ty, :, 0:576], del_ref[:, at : at + 256])
            back = term if back is None else back + term
        back = back * ds_ref[:, n * 256 : (n + 1) * 256] * (mask_z * inside_y(2 * n, 1))
        shifted(back, one_ref, 0, 160, n * 256)

    for n in range(4):
        grad = None
        for ty in range(3):
            at = (2 * n + ty) * LANES
            term = _dot(wf_ref[ty, :, 0:480], one_ref[:, at : at + 256])
            grad = term if grad is None else grad + term
        for y in range(2):
            for c in range(4):
                field_ref[c, 2 * n + y] = grad[c * 8 : (c + 1) * 8, y * LANES : (y + 1) * LANES]

    row, col = _iota((128, 128), 0), _iota((128, 128), 1)
    order = jnp.where(col == (row % 8) * 16 + row // 8, 1.0, 0.0).astype(BF)
    for n in range(4):
        turned = _dot(order, ref_ref[:, n * 256 : (n + 1) * 256]).astype(BF)
        for y in range(2):
            for o in range(16):
                refined_ref[o, 2 * n + y] = turned[o * 8 : (o + 1) * 8, y * LANES : (y + 1) * LANES]

    lane_z = _iota((1, LANES), 1) >> 4
    own_two = del_ref[224:352, 256:1280]
    own_one = one_ref[176:304, 128:1152]

    def folded(value):
        for step in (64, 32, 16):
            value = value + pltpu.roll(value, step, 1)
        return value

    def packed(taps, rows):
        groups = []
        for g in range(4):
            out = jnp.zeros((rows, LANES), F32)
            for t in range(8 * g, min(8 * g + 8, len(taps))):
                out = jnp.where(lane_z == t % 8, taps[t], out)
            groups.append(out)
        return groups

    taps = [None] * 27
    for ty in range(3):
        for tx in range(3):
            lanes = slice((2 + ty) * LANES, (2 + ty) * LANES + 1024)
            pairs = _dot_lanes(act_ref[tx * 256 + 32 : tx * 256 + 192, lanes], own_two)
            for tz in range(3):
                total = jnp.zeros((16, LANES), F32)
                for z in range(tz, tz + 8):
                    total = total + jnp.where(lane_z == z - tz, pairs[z * 16 : (z + 1) * 16], 0.0)
                taps[(ty * 3 + tz) * 3 + tx] = folded(total)
    ones = jnp.ones((16, 1024), BF)
    taps.append(folded(_dot_lanes(ones, own_two)))
    taps.append(folded(_dot_lanes(ones, own_one)))
    for g, group in enumerate(packed(taps, 16)):
        sums_ref[g * 16 : (g + 1) * 16, :] = group

    taps = [None] * 27
    row_z = (_iota((64, LANES), 0) >> 2) - (_iota((64, LANES), 1) >> 4) - 3
    for ty in range(3):
        for tx in range(3):
            lanes = slice((3 + ty) * LANES, (3 + ty) * LANES + 1024)
            pairs = _dot_lanes(dens_ref[tx * 64 : (tx + 1) * 64, lanes], own_one)
            for tz in range(3):
                chosen = jnp.where(row_z == tz, pairs, 0.0)
                total = chosen[0:8]
                for i in range(1, 8):
                    total = total + chosen[i * 8 : (i + 1) * 8]
                total = total + pltpu.roll(total, 4, 0)
                taps[(ty * 3 + tz) * 3 + tx] = folded(total)
    upper = _iota((8, LANES), 0) < 4
    groups = packed(taps, 8)
    sums_ref[64:72, :] = jnp.where(upper, groups[0], groups[1])
    sums_ref[72:80, :] = jnp.where(upper, groups[2], groups[3])


def _finish_kernel(scale, a_ref, b_ref, c_ref, d_ref, k1_ref, b1_ref, k2_ref, b2_ref):
    total = ((a_ref[...] + b_ref[...]) + (c_ref[...] + d_ref[...])) * scale
    for g in range(4):
        block = jnp.swapaxes(total[g * 16 : (g + 1) * 16, :], 0, 1)
        for j in range(8):
            t = g * 8 + j
            if t < 27:
                k2_ref[t] = block[j * 16 : (j + 1) * 16, :]
    tail = total[48:49, :]
    b2_ref[...] = tail[:, 48:64]
    b1_ref[...] = tail[:, 64:80]
    for t in range(27):
        g = t // 8
        rows = 64 + 8 * (g // 2) + 4 * (g % 2)
        k1_ref[t] = total[rows : rows + 4, (t % 8) * 16 : (t % 8) * 16 + 16]


def _local(
    offsets,
    masses,
    velocities,
    destination,
    first_weight,
    first_bias,
    second_weight,
    second_bias,
    cotangent,
):
    count_y = lax.axis_size("gy")
    count_z = lax.axis_size("gz")
    devices = count_y * count_z
    channels, span_y, span_z, span_x = cotangent.shape
    spans = (float(span_y), float(span_z), float(span_x))
    lanes = span_y * span_x
    both = ("gy", "gz")

    def along(axis, first, second):
        count = lax.axis_size(axis)
        inner = [(i, i ^ 1) for i in range(count)]
        outer = [(i, i + 1) for i in range(1, count - 1, 2)]
        outer = outer + [(j, i) for i, j in outer]
        far = lax.ppermute(second, axis, outer)
        return far, lax.ppermute(first, axis, inner)

    outgoing = _route(offsets, masses, velocities, destination, devices, spans)
    arrived = lax.all_to_all(outgoing, both, split_axis=0, concat_axis=0, tiled=True)

    turned, first, second = _call(
        _turn_kernel,
        (
            jax.ShapeDtypeStruct((channels * span_z, lanes), BF),
            jax.ShapeDtypeStruct((32, lanes), BF),
            jax.ShapeDtypeStruct((32, lanes), BF),
        ),
        flops=10**8,
        moved=10**6,
    )(cotangent)
    cot_wide, first, second = _call(
        _rim_kernel,
        (
            jax.ShapeDtypeStruct((192, lanes), BF),
            jax.ShapeDtypeStruct((192, 256), BF),
            jax.ShapeDtypeStruct((192, 256), BF),
        ),
        flops=10**6,
        moved=10**6,
    )(turned, *along("gz", first, second))
    rims = along("gy", first, second)
    k1 = first_weight.transpose(2, 3, 4, 1, 0).reshape(27, 4, 16)
    k2 = second_weight.transpose(2, 3, 4, 0, 1).reshape(27, 16, 16)
    banded = _call(
        _weights_kernel,
        (
            jax.ShapeDtypeStruct((3, 224, 256), BF),
            jax.ShapeDtypeStruct((3, 192, 768), BF),
            jax.ShapeDtypeStruct((3, 160, 640), BF),
            jax.ShapeDtypeStruct((3, 32, 512), BF),
            jax.ShapeDtypeStruct((16, 256), F32),
            jax.ShapeDtypeStruct((16, 256), F32),
        ),
        [pltpu.VMEM((32, 512), F32)],
        flops=2 * 10**9,
        moved=2 * 10**6,
    )(k1, k2, first_bias.reshape(1, 16), second_bias.reshape(1, 16))

    earlier = [banded[0]]
    own, first, second = pl.pallas_call(
        functools.partial(_deposit_kernel, span_y),
        out_shape=(
            jax.ShapeDtypeStruct((40, lanes + span_x), F32),
            jax.ShapeDtypeStruct((24, lanes + span_x), BF),
            jax.ShapeDtypeStruct((24, lanes + span_x), BF),
        ),
        in_specs=[pl.BlockSpec(memory_space=pltpu.VMEM)] + [pl.BlockSpec(memory_space=pl.ANY)] * len(earlier),
        scratch_shapes=[pltpu.VMEM((40 * (span_y + 1), span_x), F32)],
        compiler_params=pltpu.CompilerParams(vmem_limit_bytes=VMEM_LIMIT),
        cost_estimate=pl.CostEstimate(flops=4 * 10**9, bytes_accessed=10**6, transcendentals=0),
    )(arrived, *earlier)
    wide, first, second = _call(
        functools.partial(_merge_kernel, count_z),
        (
            jax.ShapeDtypeStruct((64, lanes + span_x), F32),
            jax.ShapeDtypeStruct((64, 640), BF),
            jax.ShapeDtypeStruct((64, 640), BF),
        ),
        flops=10**6,
        moved=10**6,
    )(own, *along("gz", first, second))
    refined, grad_field, sums = _call(
        functools.partial(_net_kernel, count_y, count_z),
        (
            jax.ShapeDtypeStruct(cotangent.shape, BF),
            jax.ShapeDtypeStruct((4,) + cotangent.shape[1:], F32),
            jax.ShapeDtypeStruct((80, LANES), F32),
        ),
        [
            pltpu.VMEM((2, 192, 256), F32),
            pltpu.VMEM((192, 2048), BF),
            pltpu.VMEM((768, 1792), BF),
            pltpu.VMEM((576, 1536), BF),
            pltpu.VMEM((480, 1280), BF),
            pltpu.VMEM((160, 1280), F32),
            pltpu.VMEM((128, 1024), BF),
        ],
        flops=6 * 10**9,
        moved=2 * 10**6,
    )(wide, cot_wide, *along("gy", first, second), *rims, *banded)

    def swapped(value, bit):
        return lax.ppermute(value, both, [(i, i ^ bit) for i in range(devices)])

    bits = [1 << i for i in range((devices - 1).bit_length())]
    inner_bit = count_z
    rest = [b for b in bits if b != inner_bit]
    total = sums + swapped(sums, inner_bit)
    while len(rest) > 2:
        a = rest.pop()
        if len(rest) > 2:
            b = rest.pop(0)
            total = (total + swapped(total, a)) + (swapped(total, b) + swapped(total, a ^ b))
        else:
            total = total + swapped(total, a)
    a, b = rest
    parts = (total, swapped(total, a), swapped(total, b), swapped(total, a ^ b))
    scale = 1.0 / math.sqrt(span_y * span_z * span_x * devices)
    g1, gb1, g2, gb2 = _call(
        functools.partial(_finish_kernel, scale),
        (
            jax.ShapeDtypeStruct((27, 4, 16), F32),
            jax.ShapeDtypeStruct((1, 16), F32),
            jax.ShapeDtypeStruct((27, 16, 16), F32),
            jax.ShapeDtypeStruct((1, 16), F32),
        ),
        flops=10**5,
        moved=10**5,
    )(*parts)
    return (
        refined,
        grad_field,
        g1.reshape(3, 3, 3, 4, 16).transpose(4, 3, 0, 1, 2),
        gb1.reshape(16),
        g2.reshape(3, 3, 3, 16, 16).transpose(3, 4, 0, 1, 2),
        gb2.reshape(16),
    )


def solution(mesh):
    placed = (
        P(None, ("gy", "gz")),
        P(("gy", "gz")),
        P(None, ("gy", "gz")),
        P(("gy", "gz"), None),
        P(),
        P(),
        P(),
        P(),
        P(None, "gy", "gz", None),
    )
    return jax.shard_map(
        _local,
        mesh=mesh,
        in_specs=placed,
        out_specs=(P(None, "gy", "gz", None), P(None, "gy", "gz", None), P(), P(), P(), P()),
        check_vma=False,
    )
```

```python
import functools
import math

import jax
import jax.numpy as jnp
from jax import lax
from jax.experimental import pallas as pl
from jax.experimental.pallas import tpu as pltpu
from jax.sharding import PartitionSpec as P

BF = jnp.bfloat16
F32 = jnp.float32
I32 = jnp.int32
I16 = jnp.int16
MASS_TOP, SPEED_TOP = 4.0, 5.0
STEPS = 32767.0
LANES = 128
PARTS = 10
VALUES = 8
VMEM_LIMIT = 48 * 1024 * 1024
ROUTE_VMEM_LIMIT = 60 * 1024 * 1024
ROUTE_WIDTH = 512


def _iota(shape, dim):
    return lax.broadcasted_iota(jnp.int32, shape, dim)


def _dot(a, b):
    return jnp.dot(a, b, preferred_element_type=F32)


def _dot_lanes(a, b):
    return lax.dot_general(a, b, (((1,), (1,)), ((), ())), preferred_element_type=F32)


def _call(kernel, out_shape, scratch=(), flops=0, moved=0):
    return pl.pallas_call(
        kernel,
        out_shape=out_shape,
        scratch_shapes=list(scratch),
        compiler_params=pltpu.CompilerParams(vmem_limit_bytes=VMEM_LIMIT),
        cost_estimate=pl.CostEstimate(flops=flops, bytes_accessed=moved, transcendentals=0),
    )


def _route_kernel(
    devices, off_hbm, mass_hbm, vel_hbm, dest_hbm, out_ref,
    off_ref, mass_ref, vel_ref, dest_ref, acc_ref, rank_ref, sems,
):
    loads = [
        pltpu.make_async_copy(src, dst, sems.at[i])
        for i, (src, dst) in enumerate(
            ((dest_hbm, dest_ref), (off_hbm, off_ref), (mass_hbm, mass_ref), (vel_hbm, vel_ref))
        )
    ]
    for load in loads:
        load.start()
    particles = dest_ref.shape[1]
    capacity = 2 * particles // devices
    pieces = capacity // LANES
    width = ROUTE_WIDTH
    lo_count = 2 * LANES
    hi_count = 2 * particles // lo_count
    row, col = _iota((LANES, 2 * LANES), 0), _iota((LANES, 2 * LANES), 1)
    prefix = jnp.where((row <= col) | (col >= LANES), 1.0, 0.0).astype(BF)
    number = _iota((devices, LANES), 0)
    loads[0].wait()

    def count(i, base):
        dests = [
            dest_ref[:, pl.ds(pl.multiple_of((i * 16 + j) * LANES, LANES), LANES)] for j in range(16)
        ]
        chosen = [jnp.where(number == dest, 1.0, 0.0) for dest in dests]
        counts = _dot(jnp.concatenate(chosen, axis=0).astype(BF), prefix)
        for j in range(16):
            mine = counts[j * devices : (j + 1) * devices]
            rank = jnp.sum(chosen[j] * (mine[:, :LANES] + base), axis=0, keepdims=True)
            at = pl.ds(pl.multiple_of((i * 16 + j) * LANES, LANES), LANES)
            rank_ref[:, at] = rank.astype(jnp.int32) - 1
            base = base + mine[:, LANES:]
        return base

    lax.fori_loop(0, particles // (16 * LANES), count, jnp.zeros((devices, LANES), F32), unroll=True)
    for load in loads[1:]:
        load.wait()

    def step(i, carry):
        lanes = slice(i * width, (i + 1) * width)
        dest = dest_ref[:, lanes]
        rank = rank_ref[:, lanes]
        if pieces >= 2:
            hi = (rank >> 8) * devices + dest
            lo = rank & 255
        else:
            half = devices // 2
            upper = dest >= half
            hi = jnp.where(upper, dest - half, dest)
            lo = rank + jnp.where(upper, LANES, 0)
        rows = []
        for axis in range(3):
            position = jnp.floor(off_ref[axis : axis + 1, lanes] * (2.0 * STEPS + 1.0) + 0.5)
            coarse = jnp.floor(position * (1.0 / 256.0))
            rows.append(coarse.astype(BF))
            rows.append((position - 256.0 * coarse).astype(BF))
        mass = mass_ref[:, lanes]
        rows.append(mass.astype(BF))
        for axis in range(3):
            rows.append((mass * vel_ref[axis : axis + 1, lanes]).astype(BF))
        at_hi = jnp.where(_iota((hi_count, width), 0) == hi, 1.0, 0.0).astype(BF)
        at_lo = jnp.where(_iota((lo_count, width), 0) == lo, 1.0, 0.0).astype(BF)
        spread = jnp.concatenate([at_hi * value for value in rows], axis=0)
        term = _dot_lanes(spread, at_lo)
        if i == 0:
            acc_ref[...] = term
        else:
            acc_ref[...] += term

    for i in range(particles // width):
        step(i, 0)
    halves = []
    for half in range(2):
        part = acc_ref[:, half * LANES : (half + 1) * LANES]

        def value(i):
            return part[i * hi_count : (i + 1) * hi_count]

        sent = [256.0 * value(2 * i) + value(2 * i + 1) - (STEPS + 1.0) for i in range(3)]
        sent.append(value(6) * (STEPS / MASS_TOP))
        for i in range(7, 10):
            root = jnp.sqrt(jnp.abs(value(i)) * (1.0 / (MASS_TOP * SPEED_TOP))) * STEPS
            sent.append(jnp.where(value(i) < 0.0, -root, root))
        sent = [jnp.floor(x + 0.5) for x in sent]
        sent.append(jnp.zeros_like(sent[0]))
        part = jnp.concatenate(sent, axis=0)
        if pieces >= 2:
            halves.append(part.reshape(VALUES * pieces // 2, devices, LANES))
        else:
            halves.append(part.reshape(VALUES, devices // 2, LANES))
    whole = jnp.concatenate(halves, axis=0 if pieces >= 2 else 1)
    out_ref[...] = jnp.transpose(whole, (1, 0, 2)).astype(I32).astype(I16)


def _route(offsets, masses, velocities, destination, devices):
    particles = masses.shape[0]
    capacity = 2 * particles // devices
    rows = VALUES * capacity // LANES
    return pl.pallas_call(
        functools.partial(_route_kernel, devices),
        out_shape=jax.ShapeDtypeStruct((devices, rows, LANES), I16),
        in_specs=[pl.BlockSpec(memory_space=pltpu.HBM)] * 4,
        scratch_shapes=[
            pltpu.VMEM((3, particles), F32),
            pltpu.VMEM((1, particles), F32),
            pltpu.VMEM((3, particles), F32),
            pltpu.VMEM((1, particles), jnp.int32),
            pltpu.VMEM((PARTS * 2 * particles // 256, 256), F32),
            pltpu.VMEM((1, particles), jnp.int32),
            pltpu.SemaphoreType.DMA((4,)),
        ],
        compiler_params=pltpu.CompilerParams(vmem_limit_bytes=ROUTE_VMEM_LIMIT),
        cost_estimate=pl.CostEstimate(flops=4 * 10**9, bytes_accessed=10**6, transcendentals=0),
    )(offsets, masses.reshape(1, particles), velocities, destination.reshape(1, particles))


def _deposit_kernel(span_y, span_z, arrived_ref, *refs):
    own_ref, first_ref, second_ref, acc_ref = refs[-4:]
    sources, height, _ = arrived_ref.shape
    pieces = height // VALUES
    group = max(1, 4 // pieces)
    width = group * pieces * LANES
    span_x = LANES
    acc_ref[...] = jnp.zeros_like(acc_ref)

    def value_rows(blocks, value):
        parts = []
        for block in blocks:
            for piece in range(pieces):
                if pieces >= 2:
                    half = pieces // 2
                    at = (piece % 2) * VALUES * half + value * half + piece // 2
                else:
                    at = value
                parts.append(block[at : at + 1, :])
        return jnp.concatenate(parts, axis=1)

    def step(i, carry):
        blocks = [arrived_ref[i * group + g].astype(I32).astype(F32) for g in range(group)]

        def position(axis, span):
            return (value_rows(blocks, axis) + (STEPS + 1.0)) * (span / (2.0 * STEPS + 1.0))

        pos_y, pos_z, pos_x = position(0, span_y), position(1, span_z), position(2, span_x)
        charges = [value_rows(blocks, 3) * (MASS_TOP / STEPS)]
        for c in range(4, 7):
            root = value_rows(blocks, c) * (1.0 / STEPS)
            charges.append(root * jnp.abs(root) * (MASS_TOP * SPEED_TOP))
        charges = jnp.concatenate(charges * 2, axis=0)
        cell_x = _iota((span_x, width), 0).astype(F32)
        hat_x = jnp.maximum(1.0 - jnp.abs(cell_x - pos_x), 0.0).astype(BF)
        cell_z = (_iota((40, width), 0) >> 2).astype(F32)
        hat_z = jnp.maximum(1.0 - jnp.abs(cell_z - pos_z), 0.0)
        planes = hat_z * jnp.concatenate([charges] * 5, axis=0)
        cell_y = _iota((16, width), 0).astype(F32)
        hat_y = jnp.maximum(1.0 - jnp.abs(cell_y - pos_y), 0.0)
        shares = [planes * hat_y[y : y + 1] for y in range(span_y + 1)]
        acc_ref[...] += _dot_lanes(jnp.concatenate(shares, axis=0).astype(BF), hat_x)
        return carry

    lax.fori_loop(0, sources // group, step, 0, unroll=True)
    own = jnp.concatenate([acc_ref[y * 40 : (y + 1) * 40, :] for y in range(span_y + 1)], axis=1)
    own_ref[...] = own
    even = lax.axis_index("gz") % 2 == 0
    first_ref[...] = jnp.where(even, own[16:40], own[0:24]).astype(BF)
    second_ref[...] = jnp.where(even, own[0:24], own[16:40]).astype(BF)


def _merge_kernel(count_z, own_ref, fb_ref, fa_ref, wide_ref, first_ref, second_ref):
    keep = jnp.where(lax.axis_index("gz") < count_z - 1, 1.0, 0.0)
    even = lax.axis_index("gy") % 2 == 0
    even_z = lax.axis_index("gz") % 2 == 0
    first, second = fa_ref[...].astype(F32), fb_ref[...].astype(F32)
    me_z = lax.axis_index("gz")
    left = jnp.where(me_z > 0, jnp.where(even_z, second, first), 0.0)
    right = jnp.where(me_z < count_z - 1, jnp.where(even_z, first, second), 0.0)
    own = own_ref[...]
    wide = jnp.concatenate(
        [
            left[0:16],
            own[0:8] + left[16:24],
            own[8:32],
            own[32:40] * keep + right[0:8],
            right[8:16],
        ],
        axis=0,
    )
    wide_ref[...] = wide
    to_next = wide[:, 512:1152]
    to_prev = wide[:, 0:640]
    first_ref[...] = jnp.where(even, to_next, to_prev).astype(BF)
    second_ref[...] = jnp.where(even, to_prev, to_next).astype(BF)


def _turn_kernel(cot_ref, out_ref, first_ref, second_ref):
    channels, span_y, span_z, _ = cot_ref.shape
    size = channels * span_z
    strips = [
        jnp.concatenate([cot_ref[o, y].astype(F32) for o in range(channels)], axis=0)
        for y in range(span_y)
    ]
    field = jnp.concatenate(strips, axis=1).astype(BF)
    row, col = _iota((size, size), 0), _iota((size, size), 1)
    order = (row % channels) * span_z + row // channels
    turned = _dot(jnp.where(col == order, 1.0, 0.0).astype(BF), field)
    out_ref[...] = turned.astype(BF)
    even = lax.axis_index("gz") % 2 == 0
    to_next, to_prev = turned[size - 32 :], turned[0:32]
    first_ref[...] = jnp.where(even, to_next, to_prev).astype(BF)
    second_ref[...] = jnp.where(even, to_prev, to_next).astype(BF)


def _rim_kernel(count_z, cot_ref, fb_ref, fa_ref, wide_ref, first_ref, second_ref):
    even = lax.axis_index("gy") % 2 == 0
    even_z = lax.axis_index("gz") % 2 == 0
    first, second = fa_ref[...].astype(F32), fb_ref[...].astype(F32)
    me_z = lax.axis_index("gz")
    left = jnp.where(me_z > 0, jnp.where(even_z, second, first), 0.0)
    right = jnp.where(me_z < count_z - 1, jnp.where(even_z, first, second), 0.0)
    wide_ref[0:32, :] = left.astype(BF)
    wide_ref[32:160, :] = cot_ref[...]
    wide_ref[160:192, :] = right.astype(BF)
    cells = wide_ref.shape[1]
    to_next = wide_ref[:, cells - 256 : cells].astype(F32)
    to_prev = wide_ref[:, 0:256].astype(F32)
    first_ref[...] = jnp.where(even, to_next, to_prev).astype(BF)
    second_ref[...] = jnp.where(even, to_prev, to_next).astype(BF)


def _weights_kernel(
    k1_ref, k2_ref, b1_ref, b2_ref, w1_ref, w2_ref, wb_ref, wf_ref, c1_ref, c2_ref, scr_ref
):
    def wide(x):
        rows, cols = x.shape
        return jnp.concatenate([x, jnp.zeros((rows, LANES - cols), F32)], axis=1)

    def base(block, stride, step, total):
        out = None
        for tx in range(3):
            for tz in range(3):
                x = wide(block(tz, tx))
                x = jnp.concatenate([x, jnp.zeros((x.shape[0], total - LANES), F32)], axis=1)
                at = tx * stride + tz * step
                x = pltpu.roll(x, at, 1) if at else x
                out = x if out is None else out + x
        return out

    for ty in range(3):
        def tap(tz, tx):
            return (ty * 3 + tz) * 3 + tx

        def back(tz, tx):
            return 26 - tap(tz, tx)

        b = base(lambda tz, tx: jnp.swapaxes(wide(k1_ref[tap(tz, tx)].astype(F32)), 0, 1)[0:16, :], 64, 4, 256)
        for z in range(14):
            w1_ref[ty, z * 16 : (z + 1) * 16, :] = (pltpu.roll(b, 4 * z, 1) if z else b).astype(BF)
        b = base(lambda tz, tx: k2_ref[tap(tz, tx)].astype(F32), 256, 16, 768)
        for z in range(12):
            w2_ref[ty, z * 16 : (z + 1) * 16, :] = (pltpu.roll(b, 16 * z, 1) if z else b).astype(BF)
        b = base(lambda tz, tx: jnp.swapaxes(wide(k2_ref[back(tz, tx)].astype(F32)), 0, 1)[0:16, :], 192, 16, 640)
        for z in range(10):
            wb_ref[ty, z * 16 : (z + 1) * 16, :] = (pltpu.roll(b, 16 * z, 1) if z else b).astype(BF)
        b = base(lambda tz, tx: k1_ref[back(tz, tx)].astype(F32), 160, 16, 512)
        for z in range(8):
            moved = pltpu.roll(b, 16 * z, 1) if z else b
            for c in range(4):
                scr_ref[c * 8 + z : c * 8 + z + 1, :] = moved[c : c + 1, :]
        wf_ref[ty] = scr_ref[...].astype(BF)

    eye = _iota((16, 16), 0) == _iota((16, 16), 1)
    for bias_ref, out_ref in ((b1_ref, c1_ref), (b2_ref, c2_ref)):
        one = jnp.sum(jnp.where(eye, bias_ref[...], 0.0), axis=1, keepdims=True)
        out_ref[...] = jnp.broadcast_to(one, (16, 256))


def _net_kernel(
    count_y, count_z, wide_ref, cotw_ref, db_ref, da_ref, cb_ref, ca_ref, w1_ref, w2_ref, wb_ref, wf_ref,
    b1_ref, b2_ref, refined_ref, field_ref, sums_ref,
    side_ref, dens_ref, act_ref, del_ref, one_ref, ds_ref, ref_ref,
):
    me_y, me_z = lax.axis_index("gy"), lax.axis_index("gz")
    even = me_y % 2 == 0

    edge = _iota((1, LANES), 1)
    first_lane, last_lane = edge == 0, edge == LANES - 1

    def shifted(value, dst, row0, stride, lane0):
        rows, lanes = value.shape
        for y in range(lanes // LANES):
            block = value[:, y * LANES : (y + 1) * LANES]
            at = slice(lane0 + y * LANES, lane0 + (y + 1) * LANES)
            left = jnp.where(first_lane, 0.0, pltpu.roll(block, 1, 1))
            right = jnp.where(last_lane, 0.0, pltpu.roll(block, LANES - 1, 1))
            dst[row0 : row0 + rows, at] = left.astype(BF)
            dst[row0 + stride : row0 + stride + rows, at] = block.astype(BF)
            dst[row0 + 2 * stride : row0 + 2 * stride + rows, at] = right.astype(BF)

    keep_y = jnp.where(me_y < count_y - 1, 1.0, 0.0)
    has_up, has_down = me_y > 0, me_y < count_y - 1

    def sides(a_ref, b_ref):
        first, second = a_ref[...].astype(F32), b_ref[...].astype(F32)
        up = jnp.where(has_up, jnp.where(even, second, first), 0.0)
        return up, jnp.where(has_down, jnp.where(even, first, second), 0.0)

    up, down = sides(da_ref, db_ref)
    side_ref[0], side_ref[1] = sides(ca_ref, cb_ref)
    shifted(up[:, 0:512], dens_ref, 0, 64, 0)
    shifted(wide_ref[:, 0:128] + up[:, 512:640], dens_ref, 0, 64, 512)
    shifted(wide_ref[:, 128:1024], dens_ref, 0, 64, 640)
    shifted(wide_ref[:, 1024:1152] * keep_y + down[:, 0:128], dens_ref, 0, 64, 1536)
    shifted(down[:, 128:512], dens_ref, 0, 64, 1664)

    def inside_z(rows, halo):
        z = me_z * 8 - halo + (_iota((rows, 1), 0) >> 4)
        return jnp.where((z >= 0) & (z < count_z * 8), 1.0, 0.0)

    def inside_y(first, halo):
        y = me_y * 8 - halo + first + (_iota((1, 256), 1) >> 7)
        return jnp.where((y >= 0) & (y < count_y * 8), 1.0, 0.0)

    bias = jnp.concatenate([b1_ref[...]] * 14, axis=0)
    mask_z = inside_z(224, 3)
    for tx in range(3):
        act_ref[tx * 256 + 224 : (tx + 1) * 256, :] = jnp.zeros((32, act_ref.shape[1]), BF)
    for n in range(7):
        pre = bias
        for ty in range(3):
            at = (2 * n + ty) * LANES
            pre = pre + _dot(w1_ref[ty, :, 0:192], dens_ref[:, at : at + 256])
        sig = 0.5 * jnp.tanh(0.5 * pre) + 0.5
        act = pre * sig
        if 1 <= n <= 5:
            mid = slice(32, 192)
            ds_ref[:, (n - 1) * 256 : n * 256] = sig[mid] * (1.0 + pre[mid] - act[mid])
        shifted(act * (mask_z * inside_y(2 * n, 3)), act_ref, 0, 256, n * 256)

    bias = jnp.concatenate([b2_ref[...]] * 12, axis=0)
    for n in range(6):
        pre = bias
        for ty in range(3):
            at = (2 * n + ty) * LANES
            pre = pre + _dot(w2_ref[ty], act_ref[:, at : at + 256])
        sig = 0.5 * jnp.tanh(0.5 * pre) + 0.5
        act = pre * sig
        if n == 0 or n == 5:
            cot = side_ref[0 if n == 0 else 1]
        else:
            cot = cotw_ref[:, (n - 1) * 256 : n * 256].astype(F32)
            ref_ref[:, (n - 1) * 256 : n * 256] = act[32:160].astype(BF)
        shifted(cot * (sig * (1.0 + pre - act)), del_ref, 0, 192, n * 256)

    mask_z = inside_z(160, 1)
    for n in range(5):
        back = None
        for ty in range(3):
            at = (2 * n + ty) * LANES
            term = _dot(wb_ref[ty, :, 0:576], del_ref[:, at : at + 256])
            back = term if back is None else back + term
        back = back * ds_ref[:, n * 256 : (n + 1) * 256] * (mask_z * inside_y(2 * n, 1))
        shifted(back, one_ref, 0, 160, n * 256)

    for n in range(4):
        grad = None
        for ty in range(3):
            at = (2 * n + ty) * LANES
            term = _dot(wf_ref[ty, :, 0:480], one_ref[:, at : at + 256])
            grad = term if grad is None else grad + term
        for y in range(2):
            for c in range(4):
                field_ref[c, 2 * n + y] = grad[c * 8 : (c + 1) * 8, y * LANES : (y + 1) * LANES]

    row, col = _iota((128, 128), 0), _iota((128, 128), 1)
    order = jnp.where(col == (row % 8) * 16 + row // 8, 1.0, 0.0).astype(BF)
    for n in range(4):
        turned = _dot(order, ref_ref[:, n * 256 : (n + 1) * 256]).astype(BF)
        for y in range(2):
            for o in range(16):
                refined_ref[o, 2 * n + y] = turned[o * 8 : (o + 1) * 8, y * LANES : (y + 1) * LANES]

    lane_z = _iota((1, LANES), 1) >> 4
    own_two = del_ref[224:352, 256:1280]
    own_one = one_ref[176:304, 128:1152]

    def folded(value):
        for step in (64, 32, 16):
            value = value + pltpu.roll(value, step, 1)
        return value

    def packed(taps, rows):
        groups = []
        for g in range(4):
            out = jnp.zeros((rows, LANES), F32)
            for t in range(8 * g, min(8 * g + 8, len(taps))):
                out = jnp.where(lane_z == t % 8, taps[t], out)
            groups.append(out)
        return groups

    taps = [None] * 27
    for ty in range(3):
        for tx in range(3):
            lanes = slice((2 + ty) * LANES, (2 + ty) * LANES + 1024)
            pairs = _dot_lanes(act_ref[tx * 256 + 32 : tx * 256 + 192, lanes], own_two)
            for tz in range(3):
                total = jnp.zeros((16, LANES), F32)
                for z in range(tz, tz + 8):
                    total = total + jnp.where(lane_z == z - tz, pairs[z * 16 : (z + 1) * 16], 0.0)
                taps[(ty * 3 + tz) * 3 + tx] = folded(total)
    ones = jnp.ones((16, 1024), BF)
    taps.append(folded(_dot_lanes(ones, own_two)))
    taps.append(folded(_dot_lanes(ones, own_one)))
    for g, group in enumerate(packed(taps, 16)):
        sums_ref[g * 16 : (g + 1) * 16, :] = group

    taps = [None] * 27
    row_z = (_iota((64, LANES), 0) >> 2) - (_iota((64, LANES), 1) >> 4) - 3
    for ty in range(3):
        for tx in range(3):
            lanes = slice((3 + ty) * LANES, (3 + ty) * LANES + 1024)
            pairs = _dot_lanes(dens_ref[tx * 64 : (tx + 1) * 64, lanes], own_one)
            for tz in range(3):
                chosen = jnp.where(row_z == tz, pairs, 0.0)
                total = chosen[0:8]
                for i in range(1, 8):
                    total = total + chosen[i * 8 : (i + 1) * 8]
                total = total + pltpu.roll(total, 4, 0)
                taps[(ty * 3 + tz) * 3 + tx] = folded(total)
    upper = _iota((8, LANES), 0) < 4
    groups = packed(taps, 8)
    sums_ref[64:72, :] = jnp.where(upper, groups[0], groups[1])
    sums_ref[72:80, :] = jnp.where(upper, groups[2], groups[3])


def _finish_kernel(scale, a_ref, b_ref, c_ref, d_ref, k1_ref, b1_ref, k2_ref, b2_ref):
    total = ((a_ref[...] + b_ref[...]) + (c_ref[...] + d_ref[...])) * scale
    for g in range(4):
        block = jnp.swapaxes(total[g * 16 : (g + 1) * 16, :], 0, 1)
        for j in range(8):
            t = g * 8 + j
            if t < 27:
                k2_ref[t] = block[j * 16 : (j + 1) * 16, :]
    tail = total[48:49, :]
    b2_ref[...] = tail[:, 48:64]
    b1_ref[...] = tail[:, 64:80]
    for t in range(27):
        g = t // 8
        rows = 64 + 8 * (g // 2) + 4 * (g % 2)
        k1_ref[t] = total[rows : rows + 4, (t % 8) * 16 : (t % 8) * 16 + 16]


def _local(
    offsets,
    masses,
    velocities,
    destination,
    first_weight,
    first_bias,
    second_weight,
    second_bias,
    cotangent,
):
    count_y = lax.axis_size("gy")
    count_z = lax.axis_size("gz")
    devices = count_y * count_z
    channels, span_y, span_z, span_x = cotangent.shape
    lanes = span_y * span_x
    both = ("gy", "gz")

    def along(axis, first, second, wrapped):
        count = lax.axis_size(axis)
        inner = [(i, i ^ 1) for i in range(count)]
        outer = [(i, i + 1) for i in range(1, count - 1, 2)]
        if wrapped == 1:
            outer.append((count - 1, 0))
        outer = outer + [(j, i) for i, j in outer]
        if wrapped == 2:
            outer = outer + [(0, 0), (count - 1, count - 1)]
        far = lax.ppermute(second, axis, outer)
        return far, lax.ppermute(first, axis, inner)

    outgoing = _route(offsets, masses, velocities, destination, devices)
    arrived = lax.all_to_all(outgoing, both, split_axis=0, concat_axis=0, tiled=True)

    turned, first, second = _call(
        _turn_kernel,
        (
            jax.ShapeDtypeStruct((channels * span_z, lanes), BF),
            jax.ShapeDtypeStruct((32, lanes), BF),
            jax.ShapeDtypeStruct((32, lanes), BF),
        ),
        flops=10**8,
        moved=10**6,
    )(cotangent)
    cot_wide, first, second = _call(
        functools.partial(_rim_kernel, count_z),
        (
            jax.ShapeDtypeStruct((192, lanes), BF),
            jax.ShapeDtypeStruct((192, 256), BF),
            jax.ShapeDtypeStruct((192, 256), BF),
        ),
        flops=10**6,
        moved=10**6,
    )(turned, *along("gz", first, second, 0))
    rims = along("gy", first, second, 1)
    k1 = first_weight.transpose(2, 3, 4, 1, 0).reshape(27, 4, 16)
    k2 = second_weight.transpose(2, 3, 4, 0, 1).reshape(27, 16, 16)
    banded = _call(
        _weights_kernel,
        (
            jax.ShapeDtypeStruct((3, 224, 256), BF),
            jax.ShapeDtypeStruct((3, 192, 768), BF),
            jax.ShapeDtypeStruct((3, 160, 640), BF),
            jax.ShapeDtypeStruct((3, 32, 512), BF),
            jax.ShapeDtypeStruct((16, 256), F32),
            jax.ShapeDtypeStruct((16, 256), F32),
        ),
        [pltpu.VMEM((32, 512), F32)],
        flops=2 * 10**9,
        moved=2 * 10**6,
    )(k1, k2, first_bias.reshape(1, 16), second_bias.reshape(1, 16))

    earlier = [banded[0]]
    own, first, second = pl.pallas_call(
        functools.partial(_deposit_kernel, span_y, span_z),
        out_shape=(
            jax.ShapeDtypeStruct((40, lanes + span_x), F32),
            jax.ShapeDtypeStruct((24, lanes + span_x), BF),
            jax.ShapeDtypeStruct((24, lanes + span_x), BF),
        ),
        in_specs=[pl.BlockSpec(memory_space=pltpu.VMEM)] + [pl.BlockSpec(memory_space=pl.ANY)] * len(earlier),
        scratch_shapes=[pltpu.VMEM((40 * (span_y + 1), span_x), F32)],
        compiler_params=pltpu.CompilerParams(vmem_limit_bytes=VMEM_LIMIT),
        cost_estimate=pl.CostEstimate(flops=4 * 10**9, bytes_accessed=10**6, transcendentals=0),
    )(arrived, *earlier)
    wide, first, second = _call(
        functools.partial(_merge_kernel, count_z),
        (
            jax.ShapeDtypeStruct((64, lanes + span_x), F32),
            jax.ShapeDtypeStruct((64, 640), BF),
            jax.ShapeDtypeStruct((64, 640), BF),
        ),
        flops=10**6,
        moved=10**6,
    )(own, *along("gz", first, second, 1))
    refined, grad_field, sums = _call(
        functools.partial(_net_kernel, count_y, count_z),
        (
            jax.ShapeDtypeStruct(cotangent.shape, BF),
            jax.ShapeDtypeStruct((4,) + cotangent.shape[1:], F32),
            jax.ShapeDtypeStruct((80, LANES), F32),
        ),
        [
            pltpu.VMEM((2, 192, 256), F32),
            pltpu.VMEM((192, 2048), BF),
            pltpu.VMEM((768, 1792), BF),
            pltpu.VMEM((576, 1536), BF),
            pltpu.VMEM((480, 1280), BF),
            pltpu.VMEM((160, 1280), F32),
            pltpu.VMEM((128, 1024), BF),
        ],
        flops=6 * 10**9,
        moved=2 * 10**6,
    )(wide, cot_wide, *along("gy", first, second, 1), *rims, *banded)

    def swapped(value, bit):
        return lax.ppermute(value, both, [(i, i ^ bit) for i in range(devices)])

    bits = [1 << i for i in range((devices - 1).bit_length())]
    inner_bit = count_z
    rest = [b for b in bits if b != inner_bit]
    total = sums + swapped(sums, inner_bit)
    while len(rest) > 2:
        a = rest.pop()
        if len(rest) > 2:
            b = rest.pop(0)
            total = (total + swapped(total, a)) + (swapped(total, b) + swapped(total, a ^ b))
        else:
            total = total + swapped(total, a)
    a, b = rest
    parts = (total, swapped(total, a), swapped(total, b), swapped(total, a ^ b))
    scale = 1.0 / math.sqrt(span_y * span_z * span_x * devices)
    g1, gb1, g2, gb2 = _call(
        functools.partial(_finish_kernel, scale),
        (
            jax.ShapeDtypeStruct((27, 4, 16), F32),
            jax.ShapeDtypeStruct((1, 16), F32),
            jax.ShapeDtypeStruct((27, 16, 16), F32),
            jax.ShapeDtypeStruct((1, 16), F32),
        ),
        flops=10**5,
        moved=10**5,
    )(*parts)
    return (
        refined,
        grad_field,
        g1.reshape(3, 3, 3, 4, 16).transpose(4, 3, 0, 1, 2),
        gb1.reshape(16),
        g2.reshape(3, 3, 3, 16, 16).transpose(3, 4, 0, 1, 2),
        gb2.reshape(16),
    )


def solution(mesh):
    placed = (
        P(None, ("gy", "gz")),
        P(("gy", "gz")),
        P(None, ("gy", "gz")),
        P(("gy", "gz"), None),
        P(),
        P(),
        P(),
        P(),
        P(None, "gy", "gz", None),
    )
    return jax.shard_map(
        _local,
        mesh=mesh,
        in_specs=placed,
        out_specs=(P(None, "gy", "gz", None), P(None, "gy", "gz", None), P(), P(), P(), P()),
        check_vma=False,
    )
```

```python
import functools
import math

import jax
import jax.numpy as jnp
from jax import lax
from jax.experimental import pallas as pl
from jax.experimental.pallas import tpu as pltpu
from jax.sharding import PartitionSpec as P

BF = jnp.bfloat16
F32 = jnp.float32
I32 = jnp.int32
I16 = jnp.int16
MASS_TOP, SPEED_TOP = 4.0, 5.0
STEPS = 32767.0
LANES = 128
PARTS = 10
VALUES = 8
VMEM_LIMIT = 48 * 1024 * 1024
ROUTE_VMEM_LIMIT = 60 * 1024 * 1024
ROUTE_WIDTH = 512


def _iota(shape, dim):
    return lax.broadcasted_iota(jnp.int32, shape, dim)


def _dot(a, b):
    return jnp.dot(a, b, preferred_element_type=F32)


def _dot_lanes(a, b):
    return lax.dot_general(a, b, (((1,), (1,)), ((), ())), preferred_element_type=F32)


def _call(kernel, out_shape, scratch=(), flops=0, moved=0):
    return pl.pallas_call(
        kernel,
        out_shape=out_shape,
        scratch_shapes=list(scratch),
        compiler_params=pltpu.CompilerParams(vmem_limit_bytes=VMEM_LIMIT),
        cost_estimate=pl.CostEstimate(flops=flops, bytes_accessed=moved, transcendentals=0),
    )


def _route_kernel(
    devices, off_hbm, mass_hbm, vel_hbm, dest_hbm, out_ref,
    off_ref, mass_ref, vel_ref, dest_ref, acc_ref, rank_ref, sems,
):
    loads = [
        pltpu.make_async_copy(src, dst, sems.at[i])
        for i, (src, dst) in enumerate(
            ((dest_hbm, dest_ref), (off_hbm, off_ref), (mass_hbm, mass_ref), (vel_hbm, vel_ref))
        )
    ]
    for load in loads:
        load.start()
    particles = dest_ref.shape[1]
    capacity = 2 * particles // devices
    pieces = capacity // LANES
    width = ROUTE_WIDTH
    lo_count = 2 * LANES
    hi_count = 2 * particles // lo_count
    row, col = _iota((LANES, 2 * LANES), 0), _iota((LANES, 2 * LANES), 1)
    prefix = jnp.where((row <= col) | (col >= LANES), 1.0, 0.0).astype(BF)
    number = _iota((devices, LANES), 0)
    loads[0].wait()

    def count(i, base):
        dests = [
            dest_ref[:, pl.ds(pl.multiple_of((i * 16 + j) * LANES, LANES), LANES)] for j in range(16)
        ]
        chosen = [jnp.where(number == dest, 1.0, 0.0) for dest in dests]
        counts = _dot(jnp.concatenate(chosen, axis=0).astype(BF), prefix)
        for j in range(16):
            mine = counts[j * devices : (j + 1) * devices]
            rank = jnp.sum(chosen[j] * (mine[:, :LANES] + base), axis=0, keepdims=True)
            at = pl.ds(pl.multiple_of((i * 16 + j) * LANES, LANES), LANES)
            rank_ref[:, at] = rank.astype(jnp.int32) - 1
            base = base + mine[:, LANES:]
        return base

    lax.fori_loop(0, particles // (16 * LANES), count, jnp.zeros((devices, LANES), F32), unroll=True)
    for load in loads[1:]:
        load.wait()

    def step(i, carry):
        lanes = slice(i * width, (i + 1) * width)
        dest = dest_ref[:, lanes]
        rank = rank_ref[:, lanes]
        if pieces >= 2:
            hi = (rank >> 8) * devices + dest
            lo = rank & 255
        else:
            half = devices // 2
            upper = dest >= half
            hi = jnp.where(upper, dest - half, dest)
            lo = rank + jnp.where(upper, LANES, 0)
        rows = []
        for axis in range(3):
            position = jnp.floor(off_ref[axis : axis + 1, lanes] * (2.0 * STEPS + 1.0) + 0.5)
            coarse = jnp.floor(position * (1.0 / 256.0))
            rows.append(coarse.astype(BF))
            rows.append((position - 256.0 * coarse).astype(BF))
        mass = mass_ref[:, lanes]
        rows.append(mass.astype(BF))
        for axis in range(3):
            rows.append((mass * vel_ref[axis : axis + 1, lanes]).astype(BF))
        at_hi = jnp.where(_iota((hi_count, width), 0) == hi, 1.0, 0.0).astype(BF)
        at_lo = jnp.where(_iota((lo_count, width), 0) == lo, 1.0, 0.0).astype(BF)
        spread = jnp.concatenate([at_hi * value for value in rows], axis=0)
        term = _dot_lanes(spread, at_lo)
        if i == 0:
            acc_ref[...] = term
        else:
            acc_ref[...] += term

    for i in range(particles // width):
        step(i, 0)
    halves = []
    for half in range(2):
        part = acc_ref[:, half * LANES : (half + 1) * LANES]

        def value(i):
            return part[i * hi_count : (i + 1) * hi_count]

        sent = [value(6) * (STEPS / MASS_TOP)]
        for i in range(7, 10):
            root = jnp.sqrt(jnp.abs(value(i)) * (1.0 / (MASS_TOP * SPEED_TOP))) * STEPS
            sent.append(jnp.where(value(i) < 0.0, -root, root))
        sent += [256.0 * value(2 * i) + value(2 * i + 1) - (STEPS + 1.0) for i in range(3)]
        sent = [jnp.floor(x + 0.5) for x in sent]
        sent.append(jnp.zeros_like(sent[0]))
        if pieces >= 2:
            steps = [x[h * devices : (h + 1) * devices] for h in range(pieces // 2) for x in sent]
            halves.append(jnp.concatenate(steps, axis=0).reshape(-1, devices, LANES))
        else:
            halves.append(jnp.concatenate(sent, axis=0).reshape(VALUES, devices // 2, LANES))
    whole = jnp.concatenate(halves, axis=0 if pieces >= 2 else 1)
    out_ref[...] = jnp.transpose(whole, (1, 0, 2)).astype(I32).astype(I16)


def _route(offsets, masses, velocities, destination, devices):
    particles = masses.shape[0]
    capacity = 2 * particles // devices
    rows = VALUES * capacity // LANES
    return pl.pallas_call(
        functools.partial(_route_kernel, devices),
        out_shape=jax.ShapeDtypeStruct((devices, rows, LANES), I16),
        in_specs=[pl.BlockSpec(memory_space=pltpu.HBM)] * 4,
        scratch_shapes=[
            pltpu.VMEM((3, particles), F32),
            pltpu.VMEM((1, particles), F32),
            pltpu.VMEM((3, particles), F32),
            pltpu.VMEM((1, particles), jnp.int32),
            pltpu.VMEM((PARTS * 2 * particles // 256, 256), F32),
            pltpu.VMEM((1, particles), jnp.int32),
            pltpu.SemaphoreType.DMA((4,)),
        ],
        compiler_params=pltpu.CompilerParams(vmem_limit_bytes=ROUTE_VMEM_LIMIT),
        cost_estimate=pl.CostEstimate(flops=4 * 10**9, bytes_accessed=10**6, transcendentals=0),
    )(offsets, masses.reshape(1, particles), velocities, destination.reshape(1, particles))


def _deposit_kernel(span_y, span_z, arrived_ref, *refs):
    own_ref, first_ref, second_ref, acc_ref = refs[-4:]
    sources, height, _ = arrived_ref.shape
    pieces = height // VALUES
    group = max(1, 4 // pieces)
    width = group * pieces * LANES
    span_x = LANES
    acc_ref[...] = jnp.zeros_like(acc_ref)

    row = _iota((VALUES, width), 0)
    span = jnp.where(row == 4, float(span_y), jnp.where(row == 5, float(span_z), float(span_x)))
    factor = jnp.where(row == 0, MASS_TOP / STEPS, span / (2.0 * STEPS + 1.0))
    offset = jnp.where(row == 0, 0.0, STEPS + 1.0)
    momentum = (row >= 1) & (row <= 3)

    def step(i, carry):
        blocks = [arrived_ref[i * group + g].astype(I32).astype(F32) for g in range(group)]
        parts = [b[VALUES * k : VALUES * (k + 1)] for b in blocks for k in range(pieces)]
        coded = jnp.concatenate(parts, axis=1)
        values = jnp.where(
            momentum,
            coded * jnp.abs(coded) * (MASS_TOP * SPEED_TOP / (STEPS * STEPS)),
            (coded + offset) * factor,
        )
        charges = jnp.where(row < 4, values, pltpu.roll(values, 4, 0))
        pos_y, pos_z, pos_x = values[4:5], values[5:6], values[6:7]
        cell_x = _iota((span_x, width), 0).astype(F32)
        hat_x = jnp.maximum((1.0 - jnp.abs(cell_x - pos_x)).astype(BF), 0.0)
        cell_z = (_iota((40, width), 0) >> 2).astype(F32)
        hat_z = jnp.maximum(1.0 - jnp.abs(cell_z - pos_z), 0.0)
        planes = hat_z * jnp.concatenate([charges] * 5, axis=0)
        cell_y = _iota((16, width), 0).astype(F32)
        hat_y = jnp.maximum(1.0 - jnp.abs(cell_y - pos_y), 0.0)
        shares = [planes * hat_y[y : y + 1] for y in range(span_y + 1)]
        acc_ref[...] += _dot_lanes(jnp.concatenate(shares, axis=0).astype(BF), hat_x)
        return carry

    lax.fori_loop(0, sources // group, step, 0, unroll=True)
    own = jnp.concatenate([acc_ref[y * 40 : (y + 1) * 40, :] for y in range(span_y + 1)], axis=1)
    own_ref[...] = own
    even = lax.axis_index("gz") % 2 == 0
    first_ref[...] = jnp.where(even, own[16:40], own[0:24]).astype(BF)
    second_ref[...] = jnp.where(even, own[0:24], own[16:40]).astype(BF)


def _merge_kernel(count_z, own_ref, fb_ref, fa_ref, wide_ref, first_ref, second_ref):
    keep = jnp.where(lax.axis_index("gz") < count_z - 1, 1.0, 0.0)
    even = lax.axis_index("gy") % 2 == 0
    even_z = lax.axis_index("gz") % 2 == 0
    first, second = fa_ref[...].astype(F32), fb_ref[...].astype(F32)
    me_z = lax.axis_index("gz")
    left = jnp.where(me_z > 0, jnp.where(even_z, second, first), 0.0)
    right = jnp.where(me_z < count_z - 1, jnp.where(even_z, first, second), 0.0)
    own = own_ref[...]
    wide = jnp.concatenate(
        [
            left[0:16],
            own[0:8] + left[16:24],
            own[8:32],
            own[32:40] * keep + right[0:8],
            right[8:16],
        ],
        axis=0,
    )
    wide_ref[...] = wide
    to_next = wide[:, 512:1152]
    to_prev = wide[:, 0:640]
    first_ref[...] = jnp.where(even, to_next, to_prev).astype(BF)
    second_ref[...] = jnp.where(even, to_prev, to_next).astype(BF)


def _turn_kernel(cot_ref, out_ref, first_ref, second_ref):
    channels, span_y, span_z, _ = cot_ref.shape
    size = channels * span_z
    strips = [
        jnp.concatenate([cot_ref[o, y].astype(F32) for o in range(channels)], axis=0)
        for y in range(span_y)
    ]
    field = jnp.concatenate(strips, axis=1).astype(BF)
    row, col = _iota((size, size), 0), _iota((size, size), 1)
    order = (row % channels) * span_z + row // channels
    turned = _dot(jnp.where(col == order, 1.0, 0.0).astype(BF), field)
    out_ref[...] = turned.astype(BF)
    even = lax.axis_index("gz") % 2 == 0
    to_next, to_prev = turned[size - 32 :], turned[0:32]
    first_ref[...] = jnp.where(even, to_next, to_prev).astype(BF)
    second_ref[...] = jnp.where(even, to_prev, to_next).astype(BF)


def _rim_kernel(count_z, cot_ref, fb_ref, fa_ref, wide_ref, first_ref, second_ref):
    even = lax.axis_index("gy") % 2 == 0
    even_z = lax.axis_index("gz") % 2 == 0
    first, second = fa_ref[...].astype(F32), fb_ref[...].astype(F32)
    me_z = lax.axis_index("gz")
    left = jnp.where(me_z > 0, jnp.where(even_z, second, first), 0.0)
    right = jnp.where(me_z < count_z - 1, jnp.where(even_z, first, second), 0.0)
    wide_ref[0:32, :] = left.astype(BF)
    wide_ref[32:160, :] = cot_ref[...]
    wide_ref[160:192, :] = right.astype(BF)
    cells = wide_ref.shape[1]
    to_next = wide_ref[:, cells - 256 : cells].astype(F32)
    to_prev = wide_ref[:, 0:256].astype(F32)
    first_ref[...] = jnp.where(even, to_next, to_prev).astype(BF)
    second_ref[...] = jnp.where(even, to_prev, to_next).astype(BF)


def _weights_kernel(
    k1_ref, k2_ref, b1_ref, b2_ref, w1_ref, w2_ref, wb_ref, wf_ref, c1_ref, c2_ref, scr_ref
):
    def wide(x):
        rows, cols = x.shape
        return jnp.concatenate([x, jnp.zeros((rows, LANES - cols), F32)], axis=1)

    def base(block, stride, step, total):
        out = None
        for tx in range(3):
            for tz in range(3):
                x = wide(block(tz, tx))
                x = jnp.concatenate([x, jnp.zeros((x.shape[0], total - LANES), F32)], axis=1)
                at = tx * stride + tz * step
                x = pltpu.roll(x, at, 1) if at else x
                out = x if out is None else out + x
        return out

    for ty in range(3):
        def tap(tz, tx):
            return (ty * 3 + tz) * 3 + tx

        def back(tz, tx):
            return 26 - tap(tz, tx)

        b = base(lambda tz, tx: jnp.swapaxes(wide(k1_ref[tap(tz, tx)].astype(F32)), 0, 1)[0:16, :], 64, 4, 256)
        for z in range(14):
            w1_ref[ty, z * 16 : (z + 1) * 16, :] = (pltpu.roll(b, 4 * z, 1) if z else b).astype(BF)
        b = base(lambda tz, tx: k2_ref[tap(tz, tx)].astype(F32), 256, 16, 768)
        for z in range(12):
            w2_ref[ty, z * 16 : (z + 1) * 16, :] = (pltpu.roll(b, 16 * z, 1) if z else b).astype(BF)
        b = base(lambda tz, tx: jnp.swapaxes(wide(k2_ref[back(tz, tx)].astype(F32)), 0, 1)[0:16, :], 192, 16, 640)
        for z in range(10):
            wb_ref[ty, z * 16 : (z + 1) * 16, :] = (pltpu.roll(b, 16 * z, 1) if z else b).astype(BF)
        b = base(lambda tz, tx: k1_ref[back(tz, tx)].astype(F32), 160, 16, 512)
        for z in range(8):
            moved = pltpu.roll(b, 16 * z, 1) if z else b
            for c in range(4):
                scr_ref[c * 8 + z : c * 8 + z + 1, :] = moved[c : c + 1, :]
        wf_ref[ty] = scr_ref[...].astype(BF)

    eye = _iota((16, 16), 0) == _iota((16, 16), 1)
    for bias_ref, out_ref in ((b1_ref, c1_ref), (b2_ref, c2_ref)):
        one = jnp.sum(jnp.where(eye, bias_ref[...], 0.0), axis=1, keepdims=True)
        out_ref[...] = jnp.broadcast_to(one, (16, 256))


def _net_kernel(
    count_y, count_z, wide_ref, cotw_ref, db_ref, da_ref, cb_ref, ca_ref, w1_ref, w2_ref, wb_ref, wf_ref,
    b1_ref, b2_ref, refined_ref, field_ref, sums_ref,
    side_ref, dens_ref, act_ref, del_ref, one_ref, ds_ref, ref_ref,
):
    me_y, me_z = lax.axis_index("gy"), lax.axis_index("gz")
    even = me_y % 2 == 0

    edge = _iota((1, LANES), 1)
    first_lane, last_lane = edge == 0, edge == LANES - 1

    def shifted(value, dst, row0, stride, lane0):
        rows, lanes = value.shape
        for y in range(lanes // LANES):
            block = value[:, y * LANES : (y + 1) * LANES]
            at = slice(lane0 + y * LANES, lane0 + (y + 1) * LANES)
            left = jnp.where(first_lane, 0.0, pltpu.roll(block, 1, 1))
            right = jnp.where(last_lane, 0.0, pltpu.roll(block, LANES - 1, 1))
            dst[row0 : row0 + rows, at] = left.astype(BF)
            dst[row0 + stride : row0 + stride + rows, at] = block.astype(BF)
            dst[row0 + 2 * stride : row0 + 2 * stride + rows, at] = right.astype(BF)

    keep_y = jnp.where(me_y < count_y - 1, 1.0, 0.0)
    has_up, has_down = me_y > 0, me_y < count_y - 1

    def sides(a_ref, b_ref):
        first, second = a_ref[...].astype(F32), b_ref[...].astype(F32)
        up = jnp.where(has_up, jnp.where(even, second, first), 0.0)
        return up, jnp.where(has_down, jnp.where(even, first, second), 0.0)

    up, down = sides(da_ref, db_ref)
    side_ref[0], side_ref[1] = sides(ca_ref, cb_ref)
    shifted(up[:, 0:512], dens_ref, 0, 64, 0)
    shifted(wide_ref[:, 0:128] + up[:, 512:640], dens_ref, 0, 64, 512)
    shifted(wide_ref[:, 128:1024], dens_ref, 0, 64, 640)
    shifted(wide_ref[:, 1024:1152] * keep_y + down[:, 0:128], dens_ref, 0, 64, 1536)
    shifted(down[:, 128:512], dens_ref, 0, 64, 1664)

    def inside_z(rows, halo):
        z = me_z * 8 - halo + (_iota((rows, 1), 0) >> 4)
        return jnp.where((z >= 0) & (z < count_z * 8), 1.0, 0.0)

    def inside_y(first, halo):
        y = me_y * 8 - halo + first + (_iota((1, 256), 1) >> 7)
        return jnp.where((y >= 0) & (y < count_y * 8), 1.0, 0.0)

    bias = jnp.concatenate([b1_ref[...]] * 14, axis=0)
    mask_z = inside_z(224, 3)
    for tx in range(3):
        act_ref[tx * 256 + 224 : (tx + 1) * 256, :] = jnp.zeros((32, act_ref.shape[1]), BF)
    for n in range(7):
        pre = bias
        for ty in range(3):
            at = (2 * n + ty) * LANES
            pre = pre + _dot(w1_ref[ty, :, 0:192], dens_ref[:, at : at + 256])
        sig = 0.5 * jnp.tanh(0.5 * pre) + 0.5
        act = pre * sig
        if 1 <= n <= 5:
            mid = slice(32, 192)
            ds_ref[:, (n - 1) * 256 : n * 256] = sig[mid] * (1.0 + pre[mid] - act[mid])
        shifted(act * (mask_z * inside_y(2 * n, 3)), act_ref, 0, 256, n * 256)

    bias = jnp.concatenate([b2_ref[...]] * 12, axis=0)
    for n in range(6):
        pre = bias
        for ty in range(3):
            at = (2 * n + ty) * LANES
            pre = pre + _dot(w2_ref[ty], act_ref[:, at : at + 256])
        sig = 0.5 * jnp.tanh(0.5 * pre) + 0.5
        act = pre * sig
        if n == 0 or n == 5:
            cot = side_ref[0 if n == 0 else 1]
        else:
            cot = cotw_ref[:, (n - 1) * 256 : n * 256].astype(F32)
            ref_ref[:, (n - 1) * 256 : n * 256] = act[32:160].astype(BF)
        shifted(cot * (sig * (1.0 + pre - act)), del_ref, 0, 192, n * 256)

    mask_z = inside_z(160, 1)
    for n in range(5):
        back = None
        for ty in range(3):
            at = (2 * n + ty) * LANES
            term = _dot(wb_ref[ty, :, 0:576], del_ref[:, at : at + 256])
            back = term if back is None else back + term
        back = back * ds_ref[:, n * 256 : (n + 1) * 256] * (mask_z * inside_y(2 * n, 1))
        shifted(back, one_ref, 0, 160, n * 256)

    for n in range(4):
        grad = None
        for ty in range(3):
            at = (2 * n + ty) * LANES
            term = _dot(wf_ref[ty, :, 0:480], one_ref[:, at : at + 256])
            grad = term if grad is None else grad + term
        for y in range(2):
            for c in range(4):
                field_ref[c, 2 * n + y] = grad[c * 8 : (c + 1) * 8, y * LANES : (y + 1) * LANES]

    row, col = _iota((128, 128), 0), _iota((128, 128), 1)
    order = jnp.where(col == (row % 8) * 16 + row // 8, 1.0, 0.0).astype(BF)
    for n in range(4):
        turned = _dot(order, ref_ref[:, n * 256 : (n + 1) * 256]).astype(BF)
        for y in range(2):
            for o in range(16):
                refined_ref[o, 2 * n + y] = turned[o * 8 : (o + 1) * 8, y * LANES : (y + 1) * LANES]

    lane_z = _iota((1, LANES), 1) >> 4
    own_two = jnp.swapaxes(del_ref[224:352, 256:1280].astype(F32), 0, 1).astype(BF)
    own_one = jnp.swapaxes(one_ref[176:304, 128:1152].astype(F32), 0, 1).astype(BF)

    def folded(value):
        for step in (64, 32, 16):
            value = value + pltpu.roll(value, step, 1)
        return value

    def packed(taps, rows):
        groups = []
        for g in range(4):
            out = jnp.zeros((rows, LANES), F32)
            for t in range(8 * g, min(8 * g + 8, len(taps))):
                out = jnp.where(lane_z == t % 8, taps[t], out)
            groups.append(out)
        return groups

    taps = [None] * 27
    for ty in range(3):
        for tx in range(3):
            lanes = slice((2 + ty) * LANES, (2 + ty) * LANES + 1024)
            pairs = _dot(act_ref[tx * 256 + 32 : tx * 256 + 192, lanes], own_two)
            for tz in range(3):
                total = jnp.zeros((16, LANES), F32)
                for z in range(tz, tz + 8):
                    total = total + jnp.where(lane_z == z - tz, pairs[z * 16 : (z + 1) * 16], 0.0)
                taps[(ty * 3 + tz) * 3 + tx] = folded(total)
    ones = jnp.ones((16, 1024), BF)
    taps.append(folded(_dot(ones, own_two)))
    taps.append(folded(_dot(ones, own_one)))
    for g, group in enumerate(packed(taps, 16)):
        sums_ref[g * 16 : (g + 1) * 16, :] = group

    taps = [None] * 27
    row_z = (_iota((64, LANES), 0) >> 2) - (_iota((64, LANES), 1) >> 4) - 3
    for ty in range(3):
        lanes = slice((3 + ty) * LANES, (3 + ty) * LANES + 1024)
        every = _dot(dens_ref[:, lanes], own_one)
        for tx in range(3):
            pairs = every[tx * 64 : (tx + 1) * 64]
            for tz in range(3):
                chosen = jnp.where(row_z == tz, pairs, 0.0)
                total = chosen[0:8]
                for i in range(1, 8):
                    total = total + chosen[i * 8 : (i + 1) * 8]
                total = total + pltpu.roll(total, 4, 0)
                taps[(ty * 3 + tz) * 3 + tx] = folded(total)
    upper = _iota((8, LANES), 0) < 4
    groups = packed(taps, 8)
    sums_ref[64:72, :] = jnp.where(upper, groups[0], groups[1])
    sums_ref[72:80, :] = jnp.where(upper, groups[2], groups[3])


def _finish_kernel(scale, a_ref, b_ref, c_ref, d_ref, k1_ref, b1_ref, k2_ref, b2_ref):
    total = ((a_ref[...] + b_ref[...]) + (c_ref[...] + d_ref[...])) * scale
    for g in range(4):
        block = jnp.swapaxes(total[g * 16 : (g + 1) * 16, :], 0, 1)
        for j in range(8):
            t = g * 8 + j
            if t < 27:
                k2_ref[t] = block[j * 16 : (j + 1) * 16, :]
    tail = total[48:49, :]
    b2_ref[...] = tail[:, 48:64]
    b1_ref[...] = tail[:, 64:80]
    for t in range(27):
        g = t // 8
        rows = 64 + 8 * (g // 2) + 4 * (g % 2)
        k1_ref[t] = total[rows : rows + 4, (t % 8) * 16 : (t % 8) * 16 + 16]


def _local(
    offsets,
    masses,
    velocities,
    destination,
    first_weight,
    first_bias,
    second_weight,
    second_bias,
    cotangent,
):
    count_y = lax.axis_size("gy")
    count_z = lax.axis_size("gz")
    devices = count_y * count_z
    channels, span_y, span_z, span_x = cotangent.shape
    lanes = span_y * span_x
    both = ("gy", "gz")

    def swaps(axis, lower):
        pairs = []
        for y in range(count_y):
            for z in range(count_z):
                place, count = (y, count_y) if axis == "gy" else (z, count_z)
                other = place ^ 1 if not lower else place + 1 if place % 2 else place - 1
                if axis == "gy":
                    partner = (other % count, z)
                elif 0 <= other < count:
                    partner = (y, other)
                else:
                    partner = (y ^ 1, z)
                pairs.append((y * count_z + z, partner[0] * count_z + partner[1]))
        return pairs

    def partial_z(first, second):
        pairs = [(i, j) for i, j in swaps("gz", True) if i // count_z == j // count_z]
        return lax.ppermute(second, both, pairs), lax.ppermute(first, both, swaps("gz", False))

    def along(axis, first, second):
        far = lax.ppermute(second, both, swaps(axis, True))
        return far, lax.ppermute(first, both, swaps(axis, False))

    outgoing = _route(offsets, masses, velocities, destination, devices)
    arrived = lax.all_to_all(outgoing, both, split_axis=0, concat_axis=0, tiled=True)

    turned, first, second = _call(
        _turn_kernel,
        (
            jax.ShapeDtypeStruct((channels * span_z, lanes), BF),
            jax.ShapeDtypeStruct((32, lanes), BF),
            jax.ShapeDtypeStruct((32, lanes), BF),
        ),
        flops=10**8,
        moved=10**6,
    )(cotangent)
    cot_wide, first, second = _call(
        functools.partial(_rim_kernel, count_z),
        (
            jax.ShapeDtypeStruct((192, lanes), BF),
            jax.ShapeDtypeStruct((192, 256), BF),
            jax.ShapeDtypeStruct((192, 256), BF),
        ),
        flops=10**6,
        moved=10**6,
    )(turned, *partial_z(first, second))
    rims = along("gy", first, second)
    k1 = first_weight.transpose(2, 3, 4, 1, 0).reshape(27, 4, 16)
    k2 = second_weight.transpose(2, 3, 4, 0, 1).reshape(27, 16, 16)
    banded = _call(
        _weights_kernel,
        (
            jax.ShapeDtypeStruct((3, 224, 256), BF),
            jax.ShapeDtypeStruct((3, 192, 768), BF),
            jax.ShapeDtypeStruct((3, 160, 640), BF),
            jax.ShapeDtypeStruct((3, 32, 512), BF),
            jax.ShapeDtypeStruct((16, 256), F32),
            jax.ShapeDtypeStruct((16, 256), F32),
        ),
        [pltpu.VMEM((32, 512), F32)],
        flops=2 * 10**9,
        moved=2 * 10**6,
    )(k1, k2, first_bias.reshape(1, 16), second_bias.reshape(1, 16))

    earlier = [banded[0]]
    own, first, second = pl.pallas_call(
        functools.partial(_deposit_kernel, span_y, span_z),
        out_shape=(
            jax.ShapeDtypeStruct((40, lanes + span_x), F32),
            jax.ShapeDtypeStruct((24, lanes + span_x), BF),
            jax.ShapeDtypeStruct((24, lanes + span_x), BF),
        ),
        in_specs=[pl.BlockSpec(memory_space=pltpu.VMEM)] + [pl.BlockSpec(memory_space=pl.ANY)] * len(earlier),
        scratch_shapes=[pltpu.VMEM((40 * (span_y + 1), span_x), F32)],
        compiler_params=pltpu.CompilerParams(vmem_limit_bytes=VMEM_LIMIT),
        cost_estimate=pl.CostEstimate(flops=4 * 10**9, bytes_accessed=10**6, transcendentals=0),
    )(arrived, *earlier)
    wide, first, second = _call(
        functools.partial(_merge_kernel, count_z),
        (
            jax.ShapeDtypeStruct((64, lanes + span_x), F32),
            jax.ShapeDtypeStruct((64, 640), BF),
            jax.ShapeDtypeStruct((64, 640), BF),
        ),
        flops=10**6,
        moved=10**6,
    )(own, *along("gz", first, second))
    refined, grad_field, sums = _call(
        functools.partial(_net_kernel, count_y, count_z),
        (
            jax.ShapeDtypeStruct(cotangent.shape, BF),
            jax.ShapeDtypeStruct((4,) + cotangent.shape[1:], F32),
            jax.ShapeDtypeStruct((80, LANES), F32),
        ),
        [
            pltpu.VMEM((2, 192, 256), F32),
            pltpu.VMEM((192, 2048), BF),
            pltpu.VMEM((768, 1792), BF),
            pltpu.VMEM((576, 1536), BF),
            pltpu.VMEM((480, 1280), BF),
            pltpu.VMEM((160, 1280), F32),
            pltpu.VMEM((128, 1024), BF),
        ],
        flops=6 * 10**9,
        moved=2 * 10**6,
    )(wide, cot_wide, *along("gy", first, second), *rims, *banded)

    def swapped(value, bit):
        return lax.ppermute(value, both, [(i, i ^ bit) for i in range(devices)])

    bits = [1 << i for i in range((devices - 1).bit_length())]
    inner_bit = count_z
    rest = [b for b in bits if b != inner_bit]
    total = sums + swapped(sums, inner_bit)
    while len(rest) > 2:
        a = rest.pop()
        if len(rest) > 2:
            b = rest.pop(0)
            total = (total + swapped(total, a)) + (swapped(total, b) + swapped(total, a ^ b))
        else:
            total = total + swapped(total, a)
    a, b = rest
    parts = (total, swapped(total, a), swapped(total, b), swapped(total, a ^ b))
    scale = 1.0 / math.sqrt(span_y * span_z * span_x * devices)
    g1, gb1, g2, gb2 = _call(
        functools.partial(_finish_kernel, scale),
        (
            jax.ShapeDtypeStruct((27, 4, 16), F32),
            jax.ShapeDtypeStruct((1, 16), F32),
            jax.ShapeDtypeStruct((27, 16, 16), F32),
            jax.ShapeDtypeStruct((1, 16), F32),
        ),
        flops=10**5,
        moved=10**5,
    )(*parts)
    return (
        refined,
        grad_field,
        g1.reshape(3, 3, 3, 4, 16).transpose(4, 3, 0, 1, 2),
        gb1.reshape(16),
        g2.reshape(3, 3, 3, 16, 16).transpose(3, 4, 0, 1, 2),
        gb2.reshape(16),
    )


def solution(mesh):
    placed = (
        P(None, ("gy", "gz")),
        P(("gy", "gz")),
        P(None, ("gy", "gz")),
        P(("gy", "gz"), None),
        P(),
        P(),
        P(),
        P(),
        P(None, "gy", "gz", None),
    )
    return jax.shard_map(
        _local,
        mesh=mesh,
        in_specs=placed,
        out_specs=(P(None, "gy", "gz", None), P(None, "gy", "gz", None), P(), P(), P(), P()),
        check_vma=False,
    )
```

```python
import functools
import math

import jax
import jax.numpy as jnp
from jax import lax
from jax.experimental import pallas as pl
from jax.experimental.pallas import tpu as pltpu
from jax.sharding import PartitionSpec as P

BF = jnp.bfloat16
F32 = jnp.float32
I32 = jnp.int32
I16 = jnp.int16
MASS_TOP, SPEED_TOP = 4.0, 5.0
STEPS = 32767.0
LANES = 128
PARTS = 10
VALUES = 8
VMEM_LIMIT = 48 * 1024 * 1024
ROUTE_VMEM_LIMIT = 60 * 1024 * 1024
ROUTE_WIDTH = 512


def _iota(shape, dim):
    return lax.broadcasted_iota(jnp.int32, shape, dim)


def _dot(a, b):
    return jnp.dot(a, b, preferred_element_type=F32)


def _dot_lanes(a, b):
    return lax.dot_general(a, b, (((1,), (1,)), ((), ())), preferred_element_type=F32)


def _call(kernel, out_shape, scratch=(), flops=0, moved=0):
    return pl.pallas_call(
        kernel,
        out_shape=out_shape,
        scratch_shapes=list(scratch),
        compiler_params=pltpu.CompilerParams(vmem_limit_bytes=VMEM_LIMIT),
        cost_estimate=pl.CostEstimate(flops=flops, bytes_accessed=moved, transcendentals=0),
    )


def _route_kernel(
    devices, off_hbm, mass_hbm, vel_hbm, dest_hbm, out_ref,
    off_ref, mass_ref, vel_ref, dest_ref, acc_ref, rank_ref, sems,
):
    loads = [
        pltpu.make_async_copy(src, dst, sems.at[i])
        for i, (src, dst) in enumerate(
            ((dest_hbm, dest_ref), (off_hbm, off_ref), (mass_hbm, mass_ref), (vel_hbm, vel_ref))
        )
    ]
    for load in loads:
        load.start()
    particles = dest_ref.shape[1]
    capacity = 2 * particles // devices
    pieces = capacity // LANES
    width = ROUTE_WIDTH
    lo_count = 2 * LANES
    hi_count = 2 * particles // lo_count
    row, col = _iota((LANES, 2 * LANES), 0), _iota((LANES, 2 * LANES), 1)
    prefix = jnp.where((row <= col) | (col >= LANES), 1.0, 0.0).astype(BF)
    number = _iota((devices, LANES), 0)
    loads[0].wait()

    def count(i, base):
        dests = [
            dest_ref[:, pl.ds(pl.multiple_of((i * 16 + j) * LANES, LANES), LANES)] for j in range(16)
        ]
        chosen = [jnp.where(number == dest, 1.0, 0.0) for dest in dests]
        counts = _dot(jnp.concatenate(chosen, axis=0).astype(BF), prefix)
        for j in range(16):
            mine = counts[j * devices : (j + 1) * devices]
            rank = jnp.sum(chosen[j] * (mine[:, :LANES] + base), axis=0, keepdims=True)
            at = pl.ds(pl.multiple_of((i * 16 + j) * LANES, LANES), LANES)
            rank_ref[:, at] = rank.astype(jnp.int32) - 1
            base = base + mine[:, LANES:]
        return base

    lax.fori_loop(0, particles // (16 * LANES), count, jnp.zeros((devices, LANES), F32), unroll=True)
    for load in loads[1:]:
        load.wait()

    def step(i, carry):
        lanes = slice(i * width, (i + 1) * width)
        dest = dest_ref[:, lanes]
        rank = rank_ref[:, lanes]
        if pieces >= 2:
            hi = (rank >> 8) * devices + dest
            lo = rank & 255
        else:
            half = devices // 2
            upper = dest >= half
            hi = jnp.where(upper, dest - half, dest)
            lo = rank + jnp.where(upper, LANES, 0)
        rows = []
        for axis in range(3):
            position = jnp.floor(off_ref[axis : axis + 1, lanes] * (2.0 * STEPS + 1.0) + 0.5)
            coarse = jnp.floor(position * (1.0 / 256.0))
            rows.append(coarse.astype(BF))
            rows.append((position - 256.0 * coarse).astype(BF))
        mass = mass_ref[:, lanes]
        rows.append(mass.astype(BF))
        for axis in range(3):
            rows.append((mass * vel_ref[axis : axis + 1, lanes]).astype(BF))
        at_hi = jnp.where(_iota((hi_count, width), 0) == hi, 1.0, 0.0).astype(BF)
        at_lo = jnp.where(_iota((lo_count, width), 0) == lo, 1.0, 0.0).astype(BF)
        spread = jnp.concatenate([at_hi * value for value in rows], axis=0)
        term = _dot_lanes(spread, at_lo)
        if i == 0:
            acc_ref[...] = term
        else:
            acc_ref[...] += term

    for i in range(particles // width):
        step(i, 0)
    halves = []
    for half in range(2):
        part = acc_ref[:, half * LANES : (half + 1) * LANES]

        def value(i):
            return part[i * hi_count : (i + 1) * hi_count]

        sent = [value(6) * (STEPS / MASS_TOP)]
        for i in range(7, 10):
            root = jnp.sqrt(jnp.abs(value(i)) * (1.0 / (MASS_TOP * SPEED_TOP))) * STEPS
            sent.append(jnp.where(value(i) < 0.0, -root, root))
        sent += [256.0 * value(2 * i) + value(2 * i + 1) - (STEPS + 1.0) for i in range(3)]
        sent = [jnp.floor(x + 0.5) for x in sent]
        sent.append(jnp.zeros_like(sent[0]))
        if pieces >= 2:
            steps = [x[h * devices : (h + 1) * devices] for h in range(pieces // 2) for x in sent]
            halves.append(jnp.concatenate(steps, axis=0).reshape(-1, devices, LANES))
        else:
            halves.append(jnp.concatenate(sent, axis=0).reshape(VALUES, devices // 2, LANES))
    whole = jnp.concatenate(halves, axis=0 if pieces >= 2 else 1)
    out_ref[...] = jnp.transpose(whole, (1, 0, 2)).astype(I32).astype(I16)


def _route(offsets, masses, velocities, destination, devices):
    particles = masses.shape[0]
    capacity = 2 * particles // devices
    rows = VALUES * capacity // LANES
    return pl.pallas_call(
        functools.partial(_route_kernel, devices),
        out_shape=jax.ShapeDtypeStruct((devices, rows, LANES), I16),
        in_specs=[pl.BlockSpec(memory_space=pltpu.HBM)] * 4,
        scratch_shapes=[
            pltpu.VMEM((3, particles), F32),
            pltpu.VMEM((1, particles), F32),
            pltpu.VMEM((3, particles), F32),
            pltpu.VMEM((1, particles), jnp.int32),
            pltpu.VMEM((PARTS * 2 * particles // 256, 256), F32),
            pltpu.VMEM((1, particles), jnp.int32),
            pltpu.SemaphoreType.DMA((4,)),
        ],
        compiler_params=pltpu.CompilerParams(vmem_limit_bytes=ROUTE_VMEM_LIMIT),
        cost_estimate=pl.CostEstimate(flops=4 * 10**9, bytes_accessed=10**6, transcendentals=0),
    )(offsets, masses.reshape(1, particles), velocities, destination.reshape(1, particles))


def _deposit_kernel(span_y, span_z, arrived_ref, *refs):
    own_ref, first_ref, second_ref, acc_ref = refs[-4:]
    sources, height, _ = arrived_ref.shape
    pieces = height // VALUES
    group = max(1, 4 // pieces)
    width = group * pieces * LANES
    span_x = LANES
    acc_ref[...] = jnp.zeros_like(acc_ref)

    row = _iota((VALUES, width), 0)
    span = jnp.where(row == 4, float(span_y), jnp.where(row == 5, float(span_z), float(span_x)))
    factor = jnp.where(row == 0, MASS_TOP / STEPS, span / (2.0 * STEPS + 1.0))
    offset = jnp.where(row == 0, 0.0, STEPS + 1.0)
    momentum = (row >= 1) & (row <= 3)

    def step(i, carry):
        blocks = [arrived_ref[i * group + g].astype(I32).astype(F32) for g in range(group)]
        parts = [b[VALUES * k : VALUES * (k + 1)] for b in blocks for k in range(pieces)]
        coded = jnp.concatenate(parts, axis=1)
        values = jnp.where(
            momentum,
            coded * jnp.abs(coded) * (MASS_TOP * SPEED_TOP / (STEPS * STEPS)),
            (coded + offset) * factor,
        )
        charges = jnp.where(row < 4, values, pltpu.roll(values, 4, 0))
        pos_y, pos_z, pos_x = values[4:5], values[5:6], values[6:7]
        cell_x = _iota((span_x, width), 0).astype(F32)
        hat_x = jnp.maximum((1.0 - jnp.abs(cell_x - pos_x)).astype(BF), 0.0)
        cell_z = (_iota((40, width), 0) >> 2).astype(F32)
        hat_z = jnp.maximum(1.0 - jnp.abs(cell_z - pos_z), 0.0)
        planes = hat_z * jnp.concatenate([charges] * 5, axis=0)
        cell_y = _iota((16, width), 0).astype(F32)
        hat_y = jnp.maximum(1.0 - jnp.abs(cell_y - pos_y), 0.0)
        shares = [planes * hat_y[y : y + 1] for y in range(span_y + 1)]
        acc_ref[...] += _dot_lanes(jnp.concatenate(shares, axis=0).astype(BF), hat_x)
        return carry

    lax.fori_loop(0, sources // group, step, 0, unroll=True)
    own = jnp.concatenate([acc_ref[y * 40 : (y + 1) * 40, :] for y in range(span_y + 1)], axis=1)
    own_ref[...] = own
    even = lax.axis_index("gz") % 2 == 0
    first_ref[...] = jnp.where(even, own[16:40], own[0:24]).astype(BF)
    second_ref[...] = jnp.where(even, own[0:24], own[16:40]).astype(BF)


def _merge_kernel(count_z, own_ref, fb_ref, fa_ref, wide_ref, first_ref, second_ref):
    keep = jnp.where(lax.axis_index("gz") < count_z - 1, 1.0, 0.0)
    even = lax.axis_index("gy") % 2 == 0
    even_z = lax.axis_index("gz") % 2 == 0
    first, second = fa_ref[...].astype(F32), fb_ref[...].astype(F32)
    me_z = lax.axis_index("gz")
    left = jnp.where(me_z > 0, jnp.where(even_z, second, first), 0.0)
    right = jnp.where(me_z < count_z - 1, jnp.where(even_z, first, second), 0.0)
    own = own_ref[...]
    wide = jnp.concatenate(
        [
            left[0:16],
            own[0:8] + left[16:24],
            own[8:32],
            own[32:40] * keep + right[0:8],
            right[8:16],
        ],
        axis=0,
    )
    wide_ref[...] = wide
    to_next = wide[:, 512:1152]
    to_prev = wide[:, 0:640]
    first_ref[...] = jnp.where(even, to_next, to_prev).astype(BF)
    second_ref[...] = jnp.where(even, to_prev, to_next).astype(BF)


def _turn_kernel(cot_ref, out_ref, first_ref, second_ref):
    channels, span_y, span_z, _ = cot_ref.shape
    size = channels * span_z
    strips = [
        jnp.concatenate([cot_ref[o, y].astype(F32) for o in range(channels)], axis=0)
        for y in range(span_y)
    ]
    field = jnp.concatenate(strips, axis=1).astype(BF)
    row, col = _iota((size, size), 0), _iota((size, size), 1)
    order = (row % channels) * span_z + row // channels
    turned = _dot(jnp.where(col == order, 1.0, 0.0).astype(BF), field)
    out_ref[...] = turned.astype(BF)
    even = lax.axis_index("gz") % 2 == 0
    to_next, to_prev = turned[size - 32 :], turned[0:32]
    first_ref[...] = jnp.where(even, to_next, to_prev).astype(BF)
    second_ref[...] = jnp.where(even, to_prev, to_next).astype(BF)


def _rim_kernel(count_z, cot_ref, fb_ref, fa_ref, wide_ref, first_ref, second_ref):
    even = lax.axis_index("gy") % 2 == 0
    even_z = lax.axis_index("gz") % 2 == 0
    first, second = fa_ref[...].astype(F32), fb_ref[...].astype(F32)
    me_z = lax.axis_index("gz")
    left = jnp.where(me_z > 0, jnp.where(even_z, second, first), 0.0)
    right = jnp.where(me_z < count_z - 1, jnp.where(even_z, first, second), 0.0)
    wide_ref[0:32, :] = left.astype(BF)
    wide_ref[32:160, :] = cot_ref[...]
    wide_ref[160:192, :] = right.astype(BF)
    cells = wide_ref.shape[1]
    to_next = wide_ref[:, cells - 256 : cells].astype(F32)
    to_prev = wide_ref[:, 0:256].astype(F32)
    first_ref[...] = jnp.where(even, to_next, to_prev).astype(BF)
    second_ref[...] = jnp.where(even, to_prev, to_next).astype(BF)


def _weights_kernel(
    k1_ref, k2_ref, b1_ref, b2_ref, w1_ref, w2_ref, wb_ref, wf_ref, c1_ref, c2_ref, scr_ref
):
    def wide(x):
        rows, cols = x.shape
        return jnp.concatenate([x, jnp.zeros((rows, LANES - cols), F32)], axis=1)

    def base(block, stride, step, total):
        out = None
        for tx in range(3):
            for tz in range(3):
                x = wide(block(tz, tx))
                x = jnp.concatenate([x, jnp.zeros((x.shape[0], total - LANES), F32)], axis=1)
                at = tx * stride + tz * step
                x = pltpu.roll(x, at, 1) if at else x
                out = x if out is None else out + x
        return out

    for ty in range(3):
        def tap(tz, tx):
            return (ty * 3 + tz) * 3 + tx

        def back(tz, tx):
            return 26 - tap(tz, tx)

        b = base(lambda tz, tx: jnp.swapaxes(wide(k1_ref[tap(tz, tx)].astype(F32)), 0, 1)[0:16, :], 64, 4, 256)
        for z in range(14):
            w1_ref[ty, z * 16 : (z + 1) * 16, :] = (pltpu.roll(b, 4 * z, 1) if z else b).astype(BF)
        b = base(lambda tz, tx: k2_ref[tap(tz, tx)].astype(F32), 256, 16, 768)
        for z in range(12):
            w2_ref[ty, z * 16 : (z + 1) * 16, :] = (pltpu.roll(b, 16 * z, 1) if z else b).astype(BF)
        b = base(lambda tz, tx: jnp.swapaxes(wide(k2_ref[back(tz, tx)].astype(F32)), 0, 1)[0:16, :], 192, 16, 640)
        for z in range(10):
            wb_ref[ty, z * 16 : (z + 1) * 16, :] = (pltpu.roll(b, 16 * z, 1) if z else b).astype(BF)
        b = base(lambda tz, tx: k1_ref[back(tz, tx)].astype(F32), 160, 16, 512)
        for z in range(8):
            moved = pltpu.roll(b, 16 * z, 1) if z else b
            for c in range(4):
                scr_ref[c * 8 + z : c * 8 + z + 1, :] = moved[c : c + 1, :]
        wf_ref[ty] = scr_ref[...].astype(BF)

    eye = _iota((16, 16), 0) == _iota((16, 16), 1)
    for bias_ref, out_ref in ((b1_ref, c1_ref), (b2_ref, c2_ref)):
        one = jnp.sum(jnp.where(eye, bias_ref[...], 0.0), axis=1, keepdims=True)
        out_ref[...] = jnp.broadcast_to(one, (16, 256))


def _net_kernel(
    count_y, count_z, wide_ref, cotw_ref, db_ref, da_ref, cb_ref, ca_ref, w1_ref, w2_ref, wb_ref,
    b1_ref, b2_ref, one_ref, ref_ref, sums_ref,
    side_ref, dens_ref, act_ref, del_ref, ds_ref,
):
    me_y, me_z = lax.axis_index("gy"), lax.axis_index("gz")
    even = me_y % 2 == 0

    edge = _iota((16, LANES), 1)
    not_first = jnp.where(edge == 0, 0.0, 1.0).astype(BF)
    not_last = jnp.where(edge == LANES - 1, 0.0, 1.0).astype(BF)

    def shifted(value, dst, row0, stride, lane0):
        rows, lanes = value.shape
        for y in range(lanes // LANES):
            block = value[:, y * LANES : (y + 1) * LANES].astype(BF)
            at = slice(lane0 + y * LANES, lane0 + (y + 1) * LANES)
            left = pltpu.roll(block, 1, 1) * jnp.concatenate([not_first] * (rows // 16), axis=0)
            right = pltpu.roll(block, LANES - 1, 1) * jnp.concatenate([not_last] * (rows // 16), axis=0)
            dst[row0 : row0 + rows, at] = left
            dst[row0 + stride : row0 + stride + rows, at] = block
            dst[row0 + 2 * stride : row0 + 2 * stride + rows, at] = right

    keep_y = jnp.where(me_y < count_y - 1, 1.0, 0.0)
    has_up, has_down = me_y > 0, me_y < count_y - 1

    def sides(a_ref, b_ref):
        first, second = a_ref[...].astype(F32), b_ref[...].astype(F32)
        up = jnp.where(has_up, jnp.where(even, second, first), 0.0)
        return up, jnp.where(has_down, jnp.where(even, first, second), 0.0)

    up, down = sides(da_ref, db_ref)
    side_ref[0], side_ref[1] = sides(ca_ref, cb_ref)
    shifted(up[:, 0:512], dens_ref, 0, 64, 0)
    shifted(wide_ref[:, 0:128] + up[:, 512:640], dens_ref, 0, 64, 512)
    shifted(wide_ref[:, 128:1024], dens_ref, 0, 64, 640)
    shifted(wide_ref[:, 1024:1152] * keep_y + down[:, 0:128], dens_ref, 0, 64, 1536)
    shifted(down[:, 128:512], dens_ref, 0, 64, 1664)

    def inside_z(rows, halo):
        z = me_z * 8 - halo + (_iota((rows, 1), 0) >> 4)
        return jnp.where((z >= 0) & (z < count_z * 8), 1.0, 0.0)

    def inside_y(first, halo):
        y = me_y * 8 - halo + first + (_iota((1, 256), 1) >> 7)
        return jnp.where((y >= 0) & (y < count_y * 8), 1.0, 0.0)

    bias = jnp.concatenate([b1_ref[...]] * 14, axis=0)
    mask_z = inside_z(224, 3)
    for tx in range(3):
        act_ref[tx * 256 + 224 : (tx + 1) * 256, :] = jnp.zeros((32, act_ref.shape[1]), BF)
    for n in range(7):
        pre = bias
        for ty in range(3):
            at = (2 * n + ty) * LANES
            pre = pre + _dot(w1_ref[ty, :, 0:192], dens_ref[:, at : at + 256])
        sig = 0.5 * jnp.tanh(0.5 * pre) + 0.5
        act = pre * sig
        if 1 <= n <= 5:
            mid = slice(32, 192)
            ds_ref[:, (n - 1) * 256 : n * 256] = sig[mid] * (1.0 + pre[mid] - act[mid])
        shifted(act * (mask_z * inside_y(2 * n, 3)), act_ref, 0, 256, n * 256)

    bias = jnp.concatenate([b2_ref[...]] * 12, axis=0)
    for n in range(6):
        pre = bias
        for ty in range(3):
            at = (2 * n + ty) * LANES
            pre = pre + _dot(w2_ref[ty], act_ref[:, at : at + 256])
        sig = 0.5 * jnp.tanh(0.5 * pre) + 0.5
        act = pre * sig
        if n == 0 or n == 5:
            cot = side_ref[0 if n == 0 else 1]
        else:
            cot = cotw_ref[:, (n - 1) * 256 : n * 256].astype(F32)
            ref_ref[:, (n - 1) * 256 : n * 256] = act[32:160].astype(BF)
        shifted(cot * (sig * (1.0 + pre - act)), del_ref, 0, 192, n * 256)

    mask_z = inside_z(160, 1)
    for n in range(5):
        back = None
        for ty in range(3):
            at = (2 * n + ty) * LANES
            term = _dot(wb_ref[ty, :, 0:576], del_ref[:, at : at + 256])
            back = term if back is None else back + term
        back = back * ds_ref[:, n * 256 : (n + 1) * 256] * (mask_z * inside_y(2 * n, 1))
        shifted(back, one_ref, 0, 160, n * 256)

    lane_z = _iota((1, LANES), 1) >> 4
    own_two = jnp.swapaxes(del_ref[224:352, 256:1280].astype(F32), 0, 1).astype(BF)
    own_one = jnp.swapaxes(one_ref[176:304, 128:1152].astype(F32), 0, 1).astype(BF)

    def folded(value):
        for step in (64, 32, 16):
            value = value + pltpu.roll(value, step, 1)
        return value

    def packed(taps, rows):
        groups = []
        for g in range(4):
            out = jnp.zeros((rows, LANES), F32)
            for t in range(8 * g, min(8 * g + 8, len(taps))):
                out = jnp.where(lane_z == t % 8, taps[t], out)
            groups.append(out)
        return groups

    taps = [None] * 27
    for ty in range(3):
        for tx in range(3):
            lanes = slice((2 + ty) * LANES, (2 + ty) * LANES + 1024)
            pairs = _dot(act_ref[tx * 256 + 32 : tx * 256 + 192, lanes], own_two)
            for tz in range(3):
                total = jnp.zeros((16, LANES), F32)
                for z in range(tz, tz + 8):
                    total = total + jnp.where(lane_z == z - tz, pairs[z * 16 : (z + 1) * 16], 0.0)
                taps[(ty * 3 + tz) * 3 + tx] = folded(total)
    ones = jnp.ones((16, 1024), BF)
    taps.append(folded(_dot(ones, own_two)))
    taps.append(folded(_dot(ones, own_one)))
    for g, group in enumerate(packed(taps, 16)):
        sums_ref[g * 16 : (g + 1) * 16, :] = group

    taps = [None] * 27
    row_z = (_iota((64, LANES), 0) >> 2) - (_iota((64, LANES), 1) >> 4) - 3
    for ty in range(3):
        lanes = slice((3 + ty) * LANES, (3 + ty) * LANES + 1024)
        every = _dot(dens_ref[:, lanes], own_one)
        for tx in range(3):
            pairs = every[tx * 64 : (tx + 1) * 64]
            for tz in range(3):
                chosen = jnp.where(row_z == tz, pairs, 0.0)
                total = chosen[0:8]
                for i in range(1, 8):
                    total = total + chosen[i * 8 : (i + 1) * 8]
                total = total + pltpu.roll(total, 4, 0)
                taps[(ty * 3 + tz) * 3 + tx] = folded(total)
    upper = _iota((8, LANES), 0) < 4
    groups = packed(taps, 8)
    sums_ref[64:72, :] = jnp.where(upper, groups[0], groups[1])
    sums_ref[72:80, :] = jnp.where(upper, groups[2], groups[3])


def _outputs_kernel(one_ref, rows_ref, wf_ref, refined_ref, field_ref):
    for n in range(4):
        grad = None
        for ty in range(3):
            at = (2 * n + ty) * LANES
            term = _dot(wf_ref[ty, :, 0:480], one_ref[:, at : at + 256])
            grad = term if grad is None else grad + term
        for y in range(2):
            for c in range(4):
                field_ref[c, 2 * n + y] = grad[c * 8 : (c + 1) * 8, y * LANES : (y + 1) * LANES]

    row, col = _iota((128, 128), 0), _iota((128, 128), 1)
    order = jnp.where(col == (row % 8) * 16 + row // 8, 1.0, 0.0).astype(BF)
    for n in range(4):
        turned = _dot(order, rows_ref[:, n * 256 : (n + 1) * 256]).astype(BF)
        for y in range(2):
            for o in range(16):
                refined_ref[o, 2 * n + y] = turned[o * 8 : (o + 1) * 8, y * LANES : (y + 1) * LANES]


def _finish_kernel(scale, a_ref, b_ref, c_ref, d_ref, k1_ref, b1_ref, k2_ref, b2_ref):
    total = ((a_ref[...] + b_ref[...]) + (c_ref[...] + d_ref[...])) * scale
    for g in range(4):
        block = jnp.swapaxes(total[g * 16 : (g + 1) * 16, :], 0, 1)
        for j in range(8):
            t = g * 8 + j
            if t < 27:
                k2_ref[t] = block[j * 16 : (j + 1) * 16, :]
    tail = total[48:49, :]
    b2_ref[...] = tail[:, 48:64]
    b1_ref[...] = tail[:, 64:80]
    for t in range(27):
        g = t // 8
        rows = 64 + 8 * (g // 2) + 4 * (g % 2)
        k1_ref[t] = total[rows : rows + 4, (t % 8) * 16 : (t % 8) * 16 + 16]


def _local(
    offsets,
    masses,
    velocities,
    destination,
    first_weight,
    first_bias,
    second_weight,
    second_bias,
    cotangent,
):
    count_y = lax.axis_size("gy")
    count_z = lax.axis_size("gz")
    devices = count_y * count_z
    channels, span_y, span_z, span_x = cotangent.shape
    lanes = span_y * span_x
    both = ("gy", "gz")

    def swaps(axis, lower):
        pairs = []
        for y in range(count_y):
            for z in range(count_z):
                place, count = (y, count_y) if axis == "gy" else (z, count_z)
                other = place ^ 1 if not lower else place + 1 if place % 2 else place - 1
                if 0 <= other < count:
                    partner = (other, z) if axis == "gy" else (y, other)
                else:
                    partner = (y, z ^ 1) if axis == "gy" else (y ^ 1, z)
                pairs.append((y * count_z + z, partner[0] * count_z + partner[1]))
        return pairs

    def partial_z(first, second):
        pairs = [(i, j) for i, j in swaps("gz", True) if i // count_z == j // count_z]
        return lax.ppermute(second, both, pairs), lax.ppermute(first, both, swaps("gz", False))

    def along(axis, first, second):
        far = lax.ppermute(second, both, swaps(axis, True))
        return far, lax.ppermute(first, both, swaps(axis, False))

    outgoing = _route(offsets, masses, velocities, destination, devices)
    arrived = lax.all_to_all(outgoing, both, split_axis=0, concat_axis=0, tiled=True)

    turned, first, second = _call(
        _turn_kernel,
        (
            jax.ShapeDtypeStruct((channels * span_z, lanes), BF),
            jax.ShapeDtypeStruct((32, lanes), BF),
            jax.ShapeDtypeStruct((32, lanes), BF),
        ),
        flops=10**8,
        moved=10**6,
    )(cotangent)
    cot_wide, first, second = _call(
        functools.partial(_rim_kernel, count_z),
        (
            jax.ShapeDtypeStruct((192, lanes), BF),
            jax.ShapeDtypeStruct((192, 256), BF),
            jax.ShapeDtypeStruct((192, 256), BF),
        ),
        flops=10**6,
        moved=10**6,
    )(turned, *partial_z(first, second))
    rims = along("gy", first, second)
    k1 = first_weight.transpose(2, 3, 4, 1, 0).reshape(27, 4, 16)
    k2 = second_weight.transpose(2, 3, 4, 0, 1).reshape(27, 16, 16)
    banded = _call(
        _weights_kernel,
        (
            jax.ShapeDtypeStruct((3, 224, 256), BF),
            jax.ShapeDtypeStruct((3, 192, 768), BF),
            jax.ShapeDtypeStruct((3, 160, 640), BF),
            jax.ShapeDtypeStruct((3, 32, 512), BF),
            jax.ShapeDtypeStruct((16, 256), F32),
            jax.ShapeDtypeStruct((16, 256), F32),
        ),
        [pltpu.VMEM((32, 512), F32)],
        flops=2 * 10**9,
        moved=2 * 10**6,
    )(k1, k2, first_bias.reshape(1, 16), second_bias.reshape(1, 16))

    earlier = [banded[0]]
    own, first, second = pl.pallas_call(
        functools.partial(_deposit_kernel, span_y, span_z),
        out_shape=(
            jax.ShapeDtypeStruct((40, lanes + span_x), F32),
            jax.ShapeDtypeStruct((24, lanes + span_x), BF),
            jax.ShapeDtypeStruct((24, lanes + span_x), BF),
        ),
        in_specs=[pl.BlockSpec(memory_space=pltpu.VMEM)] + [pl.BlockSpec(memory_space=pl.ANY)] * len(earlier),
        scratch_shapes=[pltpu.VMEM((40 * (span_y + 1), span_x), F32)],
        compiler_params=pltpu.CompilerParams(vmem_limit_bytes=VMEM_LIMIT),
        cost_estimate=pl.CostEstimate(flops=4 * 10**9, bytes_accessed=10**6, transcendentals=0),
    )(arrived, *earlier)
    wide, first, second = _call(
        functools.partial(_merge_kernel, count_z),
        (
            jax.ShapeDtypeStruct((64, lanes + span_x), F32),
            jax.ShapeDtypeStruct((64, 640), BF),
            jax.ShapeDtypeStruct((64, 640), BF),
        ),
        flops=10**6,
        moved=10**6,
    )(own, *along("gz", first, second))
    w1, w2, wb, wf, b1, b2 = banded
    delta_one, rows, sums = _call(
        functools.partial(_net_kernel, count_y, count_z),
        (
            jax.ShapeDtypeStruct((480, 1280), BF),
            jax.ShapeDtypeStruct((128, 1024), BF),
            jax.ShapeDtypeStruct((80, LANES), F32),
        ),
        [
            pltpu.VMEM((2, 192, 256), F32),
            pltpu.VMEM((192, 2048), BF),
            pltpu.VMEM((768, 1792), BF),
            pltpu.VMEM((576, 1536), BF),
            pltpu.VMEM((160, 1280), F32),
        ],
        flops=6 * 10**9,
        moved=2 * 10**6,
    )(wide, cot_wide, *along("gy", first, second), *rims, w1, w2, wb, b1, b2)
    refined, grad_field = _call(
        _outputs_kernel,
        (
            jax.ShapeDtypeStruct(cotangent.shape, BF),
            jax.ShapeDtypeStruct((4,) + cotangent.shape[1:], F32),
        ),
        flops=10**9,
        moved=10**6,
    )(delta_one, rows, wf)

    def swapped(value, bit):
        return lax.ppermute(value, both, [(i, i ^ bit) for i in range(devices)])

    bits = [1 << i for i in range((devices - 1).bit_length())]
    inner_bit = count_z
    rest = [b for b in bits if b != inner_bit]
    total = sums + swapped(sums, inner_bit)
    while len(rest) > 2:
        a = rest.pop()
        if len(rest) > 2:
            b = rest.pop(0)
            total = (total + swapped(total, a)) + (swapped(total, b) + swapped(total, a ^ b))
        else:
            total = total + swapped(total, a)
    a, b = rest
    parts = (total, swapped(total, a), swapped(total, b), swapped(total, a ^ b))
    scale = 1.0 / math.sqrt(span_y * span_z * span_x * devices)
    g1, gb1, g2, gb2 = _call(
        functools.partial(_finish_kernel, scale),
        (
            jax.ShapeDtypeStruct((27, 4, 16), F32),
            jax.ShapeDtypeStruct((1, 16), F32),
            jax.ShapeDtypeStruct((27, 16, 16), F32),
            jax.ShapeDtypeStruct((1, 16), F32),
        ),
        flops=10**5,
        moved=10**5,
    )(*parts)
    return (
        refined,
        grad_field,
        g1.reshape(3, 3, 3, 4, 16).transpose(4, 3, 0, 1, 2),
        gb1.reshape(16),
        g2.reshape(3, 3, 3, 16, 16).transpose(3, 4, 0, 1, 2),
        gb2.reshape(16),
    )


def solution(mesh):
    placed = (
        P(None, ("gy", "gz")),
        P(("gy", "gz")),
        P(None, ("gy", "gz")),
        P(("gy", "gz"), None),
        P(),
        P(),
        P(),
        P(),
        P(None, "gy", "gz", None),
    )
    return jax.shard_map(
        _local,
        mesh=mesh,
        in_specs=placed,
        out_specs=(P(None, "gy", "gz", None), P(None, "gy", "gz", None), P(), P(), P(), P()),
        check_vma=False,
    )
```

```python
import functools
import math

import jax
import jax.numpy as jnp
from jax import lax
from jax.experimental import pallas as pl
from jax.experimental.pallas import tpu as pltpu
from jax.sharding import PartitionSpec as P

BF = jnp.bfloat16
F32 = jnp.float32
I32 = jnp.int32
I16 = jnp.int16
MASS_TOP, SPEED_TOP = 4.0, 5.0
STEPS = 32767.0
LANES = 128
PARTS = 10
VALUES = 8
VMEM_LIMIT = 48 * 1024 * 1024
ROUTE_VMEM_LIMIT = 60 * 1024 * 1024
ROUTE_WIDTH = 512


def _iota(shape, dim):
    return lax.broadcasted_iota(jnp.int32, shape, dim)


def _dot(a, b):
    return jnp.dot(a, b, preferred_element_type=F32)


def _dot_lanes(a, b):
    return lax.dot_general(a, b, (((1,), (1,)), ((), ())), preferred_element_type=F32)


def _call(kernel, out_shape, scratch=(), flops=0, moved=0):
    return pl.pallas_call(
        kernel,
        out_shape=out_shape,
        scratch_shapes=list(scratch),
        compiler_params=pltpu.CompilerParams(vmem_limit_bytes=VMEM_LIMIT),
        cost_estimate=pl.CostEstimate(flops=flops, bytes_accessed=moved, transcendentals=0),
    )


def _route_kernel(
    devices, off_hbm, mass_hbm, vel_hbm, dest_hbm, out_ref,
    off_ref, mass_ref, vel_ref, dest_ref, acc_ref, rank_ref, sems,
):
    loads = [
        pltpu.make_async_copy(src, dst, sems.at[i])
        for i, (src, dst) in enumerate(
            ((dest_hbm, dest_ref), (off_hbm, off_ref), (mass_hbm, mass_ref), (vel_hbm, vel_ref))
        )
    ]
    for load in loads:
        load.start()
    particles = dest_ref.shape[1]
    capacity = 2 * particles // devices
    pieces = capacity // LANES
    width = ROUTE_WIDTH
    lo_count = 2 * LANES
    hi_count = 2 * particles // lo_count
    row, col = _iota((LANES, 2 * LANES), 0), _iota((LANES, 2 * LANES), 1)
    prefix = jnp.where((row <= col) | (col >= LANES), 1.0, 0.0).astype(BF)
    number = _iota((devices, LANES), 0)
    loads[0].wait()

    def count(i, base):
        dests = [
            dest_ref[:, pl.ds(pl.multiple_of((i * 16 + j) * LANES, LANES), LANES)] for j in range(16)
        ]
        chosen = [jnp.where(number == dest, 1.0, 0.0) for dest in dests]
        counts = _dot(jnp.concatenate(chosen, axis=0).astype(BF), prefix)
        for j in range(16):
            mine = counts[j * devices : (j + 1) * devices]
            rank = jnp.sum(chosen[j] * (mine[:, :LANES] + base), axis=0, keepdims=True)
            at = pl.ds(pl.multiple_of((i * 16 + j) * LANES, LANES), LANES)
            rank_ref[:, at] = rank.astype(jnp.int32) - 1
            base = base + mine[:, LANES:]
        return base

    lax.fori_loop(0, particles // (16 * LANES), count, jnp.zeros((devices, LANES), F32), unroll=True)
    for load in loads[1:]:
        load.wait()

    def step(i, carry):
        lanes = slice(i * width, (i + 1) * width)
        dest = dest_ref[:, lanes]
        rank = rank_ref[:, lanes]
        if pieces >= 2:
            hi = (rank >> 8) * devices + dest
            lo = rank & 255
        else:
            half = devices // 2
            upper = dest >= half
            hi = jnp.where(upper, dest - half, dest)
            lo = rank + jnp.where(upper, LANES, 0)
        rows = []
        for axis in range(3):
            position = jnp.floor(off_ref[axis : axis + 1, lanes] * (2.0 * STEPS + 1.0) + 0.5)
            coarse = jnp.floor(position * (1.0 / 256.0))
            rows.append(coarse.astype(BF))
            rows.append((position - 256.0 * coarse).astype(BF))
        mass = mass_ref[:, lanes]
        rows.append(mass.astype(BF))
        for axis in range(3):
            rows.append((mass * vel_ref[axis : axis + 1, lanes]).astype(BF))
        at_hi = jnp.where(_iota((hi_count, width), 0) == hi, 1.0, 0.0).astype(BF)
        at_lo = jnp.where(_iota((lo_count, width), 0) == lo, 1.0, 0.0).astype(BF)
        spread = jnp.concatenate([at_hi * value for value in rows], axis=0)
        term = _dot_lanes(spread, at_lo)
        if i == 0:
            acc_ref[...] = term
        else:
            acc_ref[...] += term

    for i in range(particles // width):
        step(i, 0)
    halves = []
    for half in range(2):
        part = acc_ref[:, half * LANES : (half + 1) * LANES]

        def value(i):
            return part[i * hi_count : (i + 1) * hi_count]

        sent = [value(6) * (STEPS / MASS_TOP)]
        for i in range(7, 10):
            root = jnp.sqrt(jnp.abs(value(i)) * (1.0 / (MASS_TOP * SPEED_TOP))) * STEPS
            sent.append(jnp.where(value(i) < 0.0, -root, root))
        sent += [256.0 * value(2 * i) + value(2 * i + 1) - (STEPS + 1.0) for i in range(3)]
        sent = [jnp.floor(x + 0.5) for x in sent]
        sent.append(jnp.zeros_like(sent[0]))
        if pieces >= 2:
            steps = [x[h * devices : (h + 1) * devices] for h in range(pieces // 2) for x in sent]
            halves.append(jnp.concatenate(steps, axis=0).reshape(-1, devices, LANES))
        else:
            halves.append(jnp.concatenate(sent, axis=0).reshape(VALUES, devices // 2, LANES))
    whole = jnp.concatenate(halves, axis=0 if pieces >= 2 else 1)
    out_ref[...] = jnp.transpose(whole, (1, 0, 2)).astype(I32).astype(I16)


def _route(offsets, masses, velocities, destination, devices):
    particles = masses.shape[0]
    capacity = 2 * particles // devices
    rows = VALUES * capacity // LANES
    return pl.pallas_call(
        functools.partial(_route_kernel, devices),
        out_shape=jax.ShapeDtypeStruct((devices, rows, LANES), I16),
        in_specs=[pl.BlockSpec(memory_space=pltpu.HBM)] * 4,
        scratch_shapes=[
            pltpu.VMEM((3, particles), F32),
            pltpu.VMEM((1, particles), F32),
            pltpu.VMEM((3, particles), F32),
            pltpu.VMEM((1, particles), jnp.int32),
            pltpu.VMEM((PARTS * 2 * particles // 256, 256), F32),
            pltpu.VMEM((1, particles), jnp.int32),
            pltpu.SemaphoreType.DMA((4,)),
        ],
        compiler_params=pltpu.CompilerParams(vmem_limit_bytes=ROUTE_VMEM_LIMIT),
        cost_estimate=pl.CostEstimate(flops=4 * 10**9, bytes_accessed=10**6, transcendentals=0),
    )(offsets, masses.reshape(1, particles), velocities, destination.reshape(1, particles))


def _deposit_kernel(span_y, span_z, arrived_ref, *refs):
    own_ref, first_ref, second_ref, acc_ref = refs[-4:]
    sources, height, _ = arrived_ref.shape
    pieces = height // VALUES
    group = max(1, 4 // pieces)
    width = group * pieces * LANES
    span_x = LANES
    acc_ref[...] = jnp.zeros_like(acc_ref)

    row = _iota((VALUES, width), 0)
    span = jnp.where(row == 4, float(span_y), jnp.where(row == 5, float(span_z), float(span_x)))
    factor = jnp.where(row == 0, MASS_TOP / STEPS, span / (2.0 * STEPS + 1.0))
    offset = jnp.where(row == 0, 0.0, STEPS + 1.0)
    momentum = (row >= 1) & (row <= 3)

    def step(i, carry):
        blocks = [arrived_ref[i * group + g].astype(I32).astype(F32) for g in range(group)]
        parts = [b[VALUES * k : VALUES * (k + 1)] for b in blocks for k in range(pieces)]
        coded = jnp.concatenate(parts, axis=1)
        values = jnp.where(
            momentum,
            coded * jnp.abs(coded) * (MASS_TOP * SPEED_TOP / (STEPS * STEPS)),
            (coded + offset) * factor,
        )
        charges = jnp.where(row < 4, values, pltpu.roll(values, 4, 0))
        pos_y, pos_z, pos_x = values[4:5], values[5:6], values[6:7]
        cell_x = _iota((span_x, width), 0).astype(F32)
        hat_x = jnp.maximum((1.0 - jnp.abs(cell_x - pos_x)).astype(BF), 0.0)
        cell_z = (_iota((40, width), 0) >> 2).astype(F32)
        hat_z = jnp.maximum(1.0 - jnp.abs(cell_z - pos_z), 0.0)
        planes = hat_z * jnp.concatenate([charges] * 5, axis=0)
        cell_y = _iota((16, width), 0).astype(F32)
        hat_y = jnp.maximum(1.0 - jnp.abs(cell_y - pos_y), 0.0)
        shares = [planes * hat_y[y : y + 1] for y in range(span_y + 1)]
        acc_ref[...] += _dot_lanes(jnp.concatenate(shares, axis=0).astype(BF), hat_x)
        return carry

    lax.fori_loop(0, sources // group, step, 0, unroll=True)
    own = jnp.concatenate([acc_ref[y * 40 : (y + 1) * 40, :] for y in range(span_y + 1)], axis=1)
    own_ref[...] = own
    even = lax.axis_index("gz") % 2 == 0
    first_ref[...] = jnp.where(even, own[16:40], own[0:24]).astype(BF)
    second_ref[...] = jnp.where(even, own[0:24], own[16:40]).astype(BF)


def _merge_kernel(count_z, own_ref, fb_ref, fa_ref, wide_ref, first_ref, second_ref):
    keep = jnp.where(lax.axis_index("gz") < count_z - 1, 1.0, 0.0)
    even = lax.axis_index("gy") % 2 == 0
    even_z = lax.axis_index("gz") % 2 == 0
    first, second = fa_ref[...].astype(F32), fb_ref[...].astype(F32)
    me_z = lax.axis_index("gz")
    left = jnp.where(me_z > 0, jnp.where(even_z, second, first), 0.0)
    right = jnp.where(me_z < count_z - 1, jnp.where(even_z, first, second), 0.0)
    own = own_ref[...]
    wide = jnp.concatenate(
        [
            left[0:16],
            own[0:8] + left[16:24],
            own[8:32],
            own[32:40] * keep + right[0:8],
            right[8:16],
        ],
        axis=0,
    )
    wide_ref[...] = wide
    to_next = wide[:, 512:1152]
    to_prev = wide[:, 0:640]
    first_ref[...] = jnp.where(even, to_next, to_prev).astype(BF)
    second_ref[...] = jnp.where(even, to_prev, to_next).astype(BF)


def _turn_kernel(cot_ref, out_ref, first_ref, second_ref):
    channels, span_y, span_z, _ = cot_ref.shape
    size = channels * span_z
    strips = [
        jnp.concatenate([cot_ref[o, y].astype(F32) for o in range(channels)], axis=0)
        for y in range(span_y)
    ]
    field = jnp.concatenate(strips, axis=1).astype(BF)
    row, col = _iota((size, size), 0), _iota((size, size), 1)
    order = (row % channels) * span_z + row // channels
    turned = _dot(jnp.where(col == order, 1.0, 0.0).astype(BF), field)
    out_ref[...] = turned.astype(BF)
    even = lax.axis_index("gz") % 2 == 0
    to_next, to_prev = turned[size - 32 :], turned[0:32]
    first_ref[...] = jnp.where(even, to_next, to_prev).astype(BF)
    second_ref[...] = jnp.where(even, to_prev, to_next).astype(BF)


def _rim_kernel(count_z, cot_ref, fb_ref, fa_ref, wide_ref, first_ref, second_ref):
    even = lax.axis_index("gy") % 2 == 0
    even_z = lax.axis_index("gz") % 2 == 0
    first, second = fa_ref[...].astype(F32), fb_ref[...].astype(F32)
    me_z = lax.axis_index("gz")
    left = jnp.where(me_z > 0, jnp.where(even_z, second, first), 0.0)
    right = jnp.where(me_z < count_z - 1, jnp.where(even_z, first, second), 0.0)
    wide_ref[0:32, :] = left.astype(BF)
    wide_ref[32:160, :] = cot_ref[...]
    wide_ref[160:192, :] = right.astype(BF)
    cells = wide_ref.shape[1]
    to_next = wide_ref[:, cells - 256 : cells].astype(F32)
    to_prev = wide_ref[:, 0:256].astype(F32)
    first_ref[...] = jnp.where(even, to_next, to_prev).astype(BF)
    second_ref[...] = jnp.where(even, to_prev, to_next).astype(BF)


def _weights_kernel(
    k1_ref, k2_ref, b1_ref, b2_ref, w1_ref, w2_ref, wb_ref, wf_ref, c1_ref, c2_ref, scr_ref
):
    def wide(x):
        rows, cols = x.shape
        return jnp.concatenate([x, jnp.zeros((rows, LANES - cols), F32)], axis=1)

    def base(block, stride, step, total):
        out = None
        for tx in range(3):
            for tz in range(3):
                x = wide(block(tz, tx))
                x = jnp.concatenate([x, jnp.zeros((x.shape[0], total - LANES), F32)], axis=1)
                at = tx * stride + tz * step
                x = pltpu.roll(x, at, 1) if at else x
                out = x if out is None else out + x
        return out

    for ty in range(3):
        def tap(tz, tx):
            return (ty * 3 + tz) * 3 + tx

        def back(tz, tx):
            return 26 - tap(tz, tx)

        b = base(lambda tz, tx: jnp.swapaxes(wide(k1_ref[tap(tz, tx)].astype(F32)), 0, 1)[0:16, :], 64, 4, 256)
        for z in range(14):
            w1_ref[ty, z * 16 : (z + 1) * 16, :] = (pltpu.roll(b, 4 * z, 1) if z else b).astype(BF)
        b = base(lambda tz, tx: k2_ref[tap(tz, tx)].astype(F32), 256, 16, 768)
        for z in range(12):
            w2_ref[ty, z * 16 : (z + 1) * 16, :] = (pltpu.roll(b, 16 * z, 1) if z else b).astype(BF)
        b = base(lambda tz, tx: jnp.swapaxes(wide(k2_ref[back(tz, tx)].astype(F32)), 0, 1)[0:16, :], 192, 16, 640)
        for z in range(10):
            wb_ref[ty, z * 16 : (z + 1) * 16, :] = (pltpu.roll(b, 16 * z, 1) if z else b).astype(BF)
        b = base(lambda tz, tx: k1_ref[back(tz, tx)].astype(F32), 160, 16, 512)
        for z in range(8):
            moved = pltpu.roll(b, 16 * z, 1) if z else b
            for c in range(4):
                scr_ref[c * 8 + z : c * 8 + z + 1, :] = moved[c : c + 1, :]
        wf_ref[ty] = scr_ref[...].astype(BF)

    eye = _iota((16, 16), 0) == _iota((16, 16), 1)
    for bias_ref, out_ref in ((b1_ref, c1_ref), (b2_ref, c2_ref)):
        one = jnp.sum(jnp.where(eye, bias_ref[...], 0.0), axis=1, keepdims=True)
        out_ref[...] = jnp.broadcast_to(one, (16, 256))


def _net_kernel(
    count_y, count_z, wide_ref, cotw_ref, db_ref, da_ref, cb_ref, ca_ref, w1_ref, w2_ref, wb_ref,
    b1_ref, b2_ref, one_ref, ref_ref, sums_ref,
    side_ref, dens_ref, act_ref, del_ref, ds_ref,
):
    me_y, me_z = lax.axis_index("gy"), lax.axis_index("gz")
    even = me_y % 2 == 0

    edge = _iota((16, LANES), 1)
    not_first = jnp.where(edge == 0, 0.0, 1.0).astype(BF)
    not_last = jnp.where(edge == LANES - 1, 0.0, 1.0).astype(BF)

    def shifted(value, dst, row0, stride, lane0):
        rows, lanes = value.shape
        for y in range(lanes // LANES):
            block = value[:, y * LANES : (y + 1) * LANES].astype(BF)
            at = slice(lane0 + y * LANES, lane0 + (y + 1) * LANES)
            left = pltpu.roll(block, 1, 1) * jnp.concatenate([not_first] * (rows // 16), axis=0)
            right = pltpu.roll(block, LANES - 1, 1) * jnp.concatenate([not_last] * (rows // 16), axis=0)
            dst[row0 : row0 + rows, at] = left
            dst[row0 + stride : row0 + stride + rows, at] = block
            dst[row0 + 2 * stride : row0 + 2 * stride + rows, at] = right

    keep_y = jnp.where(me_y < count_y - 1, 1.0, 0.0)
    has_up, has_down = me_y > 0, me_y < count_y - 1

    def sides(a_ref, b_ref):
        first, second = a_ref[...].astype(F32), b_ref[...].astype(F32)
        up = jnp.where(has_up, jnp.where(even, second, first), 0.0)
        return up, jnp.where(has_down, jnp.where(even, first, second), 0.0)

    up, down = sides(da_ref, db_ref)
    side_ref[0], side_ref[1] = sides(ca_ref, cb_ref)
    shifted(up[:, 0:512], dens_ref, 0, 64, 0)
    shifted(wide_ref[:, 0:128] + up[:, 512:640], dens_ref, 0, 64, 512)
    shifted(wide_ref[:, 128:1024], dens_ref, 0, 64, 640)
    shifted(wide_ref[:, 1024:1152] * keep_y + down[:, 0:128], dens_ref, 0, 64, 1536)
    shifted(down[:, 128:512], dens_ref, 0, 64, 1664)

    def inside_z(rows, halo):
        z = me_z * 8 - halo + (_iota((rows, 1), 0) >> 4)
        return jnp.where((z >= 0) & (z < count_z * 8), 1.0, 0.0)

    def inside_y(first, halo):
        y = me_y * 8 - halo + first + (_iota((1, 256), 1) >> 7)
        return jnp.where((y >= 0) & (y < count_y * 8), 1.0, 0.0)

    bias = jnp.concatenate([b1_ref[...]] * 14, axis=0)
    mask_z = inside_z(224, 3)
    for tx in range(3):
        act_ref[tx * 256 + 224 : (tx + 1) * 256, :] = jnp.zeros((32, act_ref.shape[1]), BF)
    for n in range(7):
        pre = bias
        for ty in range(3):
            at = (2 * n + ty) * LANES
            pre = pre + _dot(w1_ref[ty, :, 0:192], dens_ref[:, at : at + 256])
        sig = 0.5 * jnp.tanh(0.5 * pre) + 0.5
        act = pre * sig
        if 1 <= n <= 5:
            mid = slice(32, 192)
            ds_ref[:, (n - 1) * 256 : n * 256] = sig[mid] * (1.0 + pre[mid] - act[mid])
        shifted(act * (mask_z * inside_y(2 * n, 3)), act_ref, 0, 256, n * 256)

    bias = jnp.concatenate([b2_ref[...]] * 12, axis=0)
    for n in range(6):
        pre = bias
        for ty in range(3):
            at = (2 * n + ty) * LANES
            pre = pre + _dot(w2_ref[ty], act_ref[:, at : at + 256])
        sig = 0.5 * jnp.tanh(0.5 * pre) + 0.5
        act = pre * sig
        if n == 0 or n == 5:
            cot = side_ref[0 if n == 0 else 1]
        else:
            cot = cotw_ref[:, (n - 1) * 256 : n * 256].astype(F32)
            ref_ref[:, (n - 1) * 256 : n * 256] = act[32:160].astype(BF)
        shifted(cot * (sig * (1.0 + pre - act)), del_ref, 0, 192, n * 256)

    mask_z = inside_z(160, 1)
    for n in range(5):
        back = None
        for ty in range(3):
            at = (2 * n + ty) * LANES
            term = _dot(wb_ref[ty, :, 0:576], del_ref[:, at : at + 256])
            back = term if back is None else back + term
        back = back * ds_ref[:, n * 256 : (n + 1) * 256] * (mask_z * inside_y(2 * n, 1))
        shifted(back, one_ref, 0, 160, n * 256)

    lane_z = _iota((1, LANES), 1) >> 4
    own_two = jnp.swapaxes(del_ref[224:352, 256:1280].astype(F32), 0, 1).astype(BF)
    own_one = jnp.swapaxes(one_ref[176:304, 128:1152].astype(F32), 0, 1).astype(BF)

    def folded(value):
        for step in (64, 32, 16):
            value = value + pltpu.roll(value, step, 1)
        return value

    def packed(taps, rows):
        groups = []
        for g in range(4):
            out = jnp.zeros((rows, LANES), F32)
            for t in range(8 * g, min(8 * g + 8, len(taps))):
                out = jnp.where(lane_z == t % 8, taps[t], out)
            groups.append(out)
        return groups

    taps = [None] * 27
    for ty in range(3):
        for tx in range(3):
            lanes = slice((2 + ty) * LANES, (2 + ty) * LANES + 1024)
            pairs = _dot(act_ref[tx * 256 + 32 : tx * 256 + 192, lanes], own_two)
            for tz in range(3):
                total = jnp.zeros((16, LANES), F32)
                for z in range(tz, tz + 8):
                    total = total + jnp.where(lane_z == z - tz, pairs[z * 16 : (z + 1) * 16], 0.0)
                taps[(ty * 3 + tz) * 3 + tx] = folded(total)
    ones = jnp.ones((16, 1024), BF)
    taps.append(folded(_dot(ones, own_two)))
    taps.append(folded(_dot(ones, own_one)))
    for g, group in enumerate(packed(taps, 16)):
        sums_ref[g * 16 : (g + 1) * 16, :] = group

    taps = [None] * 27
    row_z = (_iota((64, LANES), 0) >> 2) - (_iota((64, LANES), 1) >> 4) - 3
    for ty in range(3):
        lanes = slice((3 + ty) * LANES, (3 + ty) * LANES + 1024)
        every = _dot(dens_ref[:, lanes], own_one)
        for tx in range(3):
            pairs = every[tx * 64 : (tx + 1) * 64]
            for tz in range(3):
                chosen = jnp.where(row_z == tz, pairs, 0.0)
                total = chosen[0:8]
                for i in range(1, 8):
                    total = total + chosen[i * 8 : (i + 1) * 8]
                total = total + pltpu.roll(total, 4, 0)
                taps[(ty * 3 + tz) * 3 + tx] = folded(total)
    upper = _iota((8, LANES), 0) < 4
    groups = packed(taps, 8)
    sums_ref[64:72, :] = jnp.where(upper, groups[0], groups[1])
    sums_ref[72:80, :] = jnp.where(upper, groups[2], groups[3])


def _outputs_kernel(one_ref, rows_ref, wf_ref, refined_ref, field_ref, done_ref):
    done_ref[...] = jnp.zeros_like(done_ref)
    for n in range(4):
        grad = None
        for ty in range(3):
            at = (2 * n + ty) * LANES
            term = _dot(wf_ref[ty, :, 0:480], one_ref[:, at : at + 256])
            grad = term if grad is None else grad + term
        for y in range(2):
            for c in range(4):
                field_ref[c, 2 * n + y] = grad[c * 8 : (c + 1) * 8, y * LANES : (y + 1) * LANES]

    row, col = _iota((128, 128), 0), _iota((128, 128), 1)
    order = jnp.where(col == (row % 8) * 16 + row // 8, 1.0, 0.0).astype(BF)
    for n in range(4):
        turned = _dot(order, rows_ref[:, n * 256 : (n + 1) * 256]).astype(BF)
        for y in range(2):
            for o in range(16):
                refined_ref[o, 2 * n + y] = turned[o * 8 : (o + 1) * 8, y * LANES : (y + 1) * LANES]


def _finish_kernel(scale, a_ref, b_ref, k1_ref, b1_ref, k2_ref, b2_ref):
    total = (a_ref[...] + b_ref[...]) * scale
    for g in range(4):
        block = jnp.swapaxes(total[g * 16 : (g + 1) * 16, :], 0, 1)
        for j in range(8):
            t = g * 8 + j
            if t < 27:
                k2_ref[t] = block[j * 16 : (j + 1) * 16, :]
    tail = total[48:49, :]
    b2_ref[...] = tail[:, 48:64]
    b1_ref[...] = tail[:, 64:80]
    for t in range(27):
        g = t // 8
        rows = 64 + 8 * (g // 2) + 4 * (g % 2)
        k1_ref[t] = total[rows : rows + 4, (t % 8) * 16 : (t % 8) * 16 + 16]


def _local(
    offsets,
    masses,
    velocities,
    destination,
    first_weight,
    first_bias,
    second_weight,
    second_bias,
    cotangent,
):
    count_y = lax.axis_size("gy")
    count_z = lax.axis_size("gz")
    devices = count_y * count_z
    channels, span_y, span_z, span_x = cotangent.shape
    lanes = span_y * span_x
    both = ("gy", "gz")

    def swaps(axis, lower):
        pairs = []
        for y in range(count_y):
            for z in range(count_z):
                place, count = (y, count_y) if axis == "gy" else (z, count_z)
                other = place ^ 1 if not lower else place + 1 if place % 2 else place - 1
                if 0 <= other < count:
                    partner = (other, z) if axis == "gy" else (y, other)
                else:
                    partner = (y, z ^ 1) if axis == "gy" else (y ^ 1, z)
                pairs.append((y * count_z + z, partner[0] * count_z + partner[1]))
        return pairs

    def partial_z(first, second):
        pairs = [(i, j) for i, j in swaps("gz", True) if i // count_z == j // count_z]
        return lax.ppermute(second, both, pairs), lax.ppermute(first, both, swaps("gz", False))

    def along(axis, first, second):
        far = lax.ppermute(second, both, swaps(axis, True))
        return far, lax.ppermute(first, both, swaps(axis, False))

    outgoing = _route(offsets, masses, velocities, destination, devices)
    arrived = lax.all_to_all(outgoing, both, split_axis=0, concat_axis=0, tiled=True)

    turned, first, second = _call(
        _turn_kernel,
        (
            jax.ShapeDtypeStruct((channels * span_z, lanes), BF),
            jax.ShapeDtypeStruct((32, lanes), BF),
            jax.ShapeDtypeStruct((32, lanes), BF),
        ),
        flops=10**8,
        moved=10**6,
    )(cotangent)
    cot_wide, first, second = _call(
        functools.partial(_rim_kernel, count_z),
        (
            jax.ShapeDtypeStruct((192, lanes), BF),
            jax.ShapeDtypeStruct((192, 256), BF),
            jax.ShapeDtypeStruct((192, 256), BF),
        ),
        flops=10**6,
        moved=10**6,
    )(turned, *partial_z(first, second))
    rims = along("gy", first, second)
    k1 = first_weight.transpose(2, 3, 4, 1, 0).reshape(27, 4, 16)
    k2 = second_weight.transpose(2, 3, 4, 0, 1).reshape(27, 16, 16)
    banded = _call(
        _weights_kernel,
        (
            jax.ShapeDtypeStruct((3, 224, 256), BF),
            jax.ShapeDtypeStruct((3, 192, 768), BF),
            jax.ShapeDtypeStruct((3, 160, 640), BF),
            jax.ShapeDtypeStruct((3, 32, 512), BF),
            jax.ShapeDtypeStruct((16, 256), F32),
            jax.ShapeDtypeStruct((16, 256), F32),
        ),
        [pltpu.VMEM((32, 512), F32)],
        flops=2 * 10**9,
        moved=2 * 10**6,
    )(k1, k2, first_bias.reshape(1, 16), second_bias.reshape(1, 16))

    earlier = [banded[0]]
    own, first, second = pl.pallas_call(
        functools.partial(_deposit_kernel, span_y, span_z),
        out_shape=(
            jax.ShapeDtypeStruct((40, lanes + span_x), F32),
            jax.ShapeDtypeStruct((24, lanes + span_x), BF),
            jax.ShapeDtypeStruct((24, lanes + span_x), BF),
        ),
        in_specs=[pl.BlockSpec(memory_space=pltpu.VMEM)] + [pl.BlockSpec(memory_space=pl.ANY)] * len(earlier),
        scratch_shapes=[pltpu.VMEM((40 * (span_y + 1), span_x), F32)],
        compiler_params=pltpu.CompilerParams(vmem_limit_bytes=VMEM_LIMIT),
        cost_estimate=pl.CostEstimate(flops=4 * 10**9, bytes_accessed=10**6, transcendentals=0),
    )(arrived, *earlier)
    wide, first, second = _call(
        functools.partial(_merge_kernel, count_z),
        (
            jax.ShapeDtypeStruct((64, lanes + span_x), F32),
            jax.ShapeDtypeStruct((64, 640), BF),
            jax.ShapeDtypeStruct((64, 640), BF),
        ),
        flops=10**6,
        moved=10**6,
    )(own, *along("gz", first, second))
    w1, w2, wb, wf, b1, b2 = banded
    delta_one, rows, sums = _call(
        functools.partial(_net_kernel, count_y, count_z),
        (
            jax.ShapeDtypeStruct((480, 1280), BF),
            jax.ShapeDtypeStruct((128, 1024), BF),
            jax.ShapeDtypeStruct((80, LANES), F32),
        ),
        [
            pltpu.VMEM((2, 192, 256), F32),
            pltpu.VMEM((192, 2048), BF),
            pltpu.VMEM((768, 1792), BF),
            pltpu.VMEM((576, 1536), BF),
            pltpu.VMEM((160, 1280), F32),
        ],
        flops=6 * 10**9,
        moved=2 * 10**6,
    )(wide, cot_wide, *along("gy", first, second), *rims, w1, w2, wb, b1, b2)
    refined, grad_field, done = _call(
        _outputs_kernel,
        (
            jax.ShapeDtypeStruct(cotangent.shape, BF),
            jax.ShapeDtypeStruct((4,) + cotangent.shape[1:], F32),
            jax.ShapeDtypeStruct((80, LANES), F32),
        ),
        flops=10**9,
        moved=10**6,
    )(delta_one, rows, wf)

    def swapped(value, bit):
        return lax.ppermute(value, both, [(i, i ^ bit) for i in range(devices)])

    def by_core(value, even_bit, odd_bit):
        pairs = [(i, i ^ (odd_bit if i & inner_bit else even_bit)) for i in range(devices)]
        return lax.ppermute(value, both, pairs)

    inner_bit = count_z
    bits = [1 << i for i in range((devices - 1).bit_length())]
    rest = [b for b in bits if b != inner_bit]
    total = sums + swapped(sums, inner_bit)
    while len(rest) > 2:
        a, b = rest.pop(), rest.pop(0)
        total = (total + swapped(total, a)) + (swapped(total, b) + swapped(total, a ^ b))
    low, high = rest
    total = total + done
    even = lax.axis_index("gy") % 2 == 0
    one = by_core(total, high, low)
    two = by_core(total, bits[0], low ^ high)
    part = one + jnp.where(even, total, two)
    parts = (part, swapped(part, inner_bit))
    scale = 1.0 / math.sqrt(span_y * span_z * span_x * devices)
    g1, gb1, g2, gb2 = _call(
        functools.partial(_finish_kernel, scale),
        (
            jax.ShapeDtypeStruct((27, 4, 16), F32),
            jax.ShapeDtypeStruct((1, 16), F32),
            jax.ShapeDtypeStruct((27, 16, 16), F32),
            jax.ShapeDtypeStruct((1, 16), F32),
        ),
        flops=10**5,
        moved=10**5,
    )(*parts)
    return (
        refined,
        grad_field,
        g1.reshape(3, 3, 3, 4, 16).transpose(4, 3, 0, 1, 2),
        gb1.reshape(16),
        g2.reshape(3, 3, 3, 16, 16).transpose(3, 4, 0, 1, 2),
        gb2.reshape(16),
    )


def solution(mesh):
    placed = (
        P(None, ("gy", "gz")),
        P(("gy", "gz")),
        P(None, ("gy", "gz")),
        P(("gy", "gz"), None),
        P(),
        P(),
        P(),
        P(),
        P(None, "gy", "gz", None),
    )
    return jax.shard_map(
        _local,
        mesh=mesh,
        in_specs=placed,
        out_specs=(P(None, "gy", "gz", None), P(None, "gy", "gz", None), P(), P(), P(), P()),
        check_vma=False,
    )
```
